768 devices in a mesh: gx: 8 (over x, z_hi), gy: 16 (over y, core), gz: 6 (over z_lo).
Axes of the slice: x: 4, y: 8, z: 12 (z_hi: 2, z_lo: 6; z = z_hi * 6 + z_lo), core: 2. Of those that a mesh axis runs over, the one named last changes fastest.
Arguments:
- positions: float32 [48, 16, 16, 3, 128], P(('gx', 'gz'), 'gy'), may hold values from 0 to 1
- masses: float32 [48, 16, 16, 128], P(('gx', 'gz'), 'gy'), may hold values from 0.2 to 2
- velocities: float32 [48, 16, 16, 3, 128], P(('gx', 'gz'), 'gy'), may hold values from -6 to 6
- tile_counts: int32 [48, 16, 16], P(('gx', 'gz'), 'gy'), may hold values from 32 to 128
- neighbour_list: int32 [48, 16, 16, 6], P(('gx', 'gz'), 'gy'), may hold values from 0 to 143, as said below
Outputs:
- kicked: float32 [48, 16, 16, 3, 128], P(('gx', 'gz'), 'gy')
The draws below stay inside these ranges and needn't reach their ends.
Inputs may be any that keep to these rules, and one draw needn't show every extreme that they name: `neighbour_list`: each entry is ((dx + 1) * 3 + dy + 1) * 16 + (t + dz) mod 16 for the tile t it belongs to, dx, dy, dz each in -1, 0, 1; the 6 entries of one tile name distinct shell tiles.
All inputs are finite; a program needn't handle non-finite values.
Results may differ from the reference program's by a relative error of at most 0.0003.
Values sent between devices are 32-bit elements; how exact they have to be, the bound alone decides.
No kernel may reach another device: no remote copies, remote signals or barrier semaphores. Data moves between devices by JAX's collectives and lax.ppermute only.
A program may use at most 64 MiB of HBM per device.

```python
import math
import jax
import jax.numpy as jnp
from jax import lax

CX = 2
CY = 6
NZ = 1024
TZ = 16
NB = 6
GRID_X = 48
GRID_Y = 16
NX = 96
NY = 96


def draw_neighbour_list(key, part):
    scores = jax.random.randint(jax.random.fold_in(key, 17), (GRID_X, GRID_Y, TZ, 27), 0, 1 << 20) * 32 + jnp.arange(27, dtype=jnp.int32)
    chosen = jnp.argsort(scores, axis=-1)[..., :NB].astype(jnp.int32)
    groups = chosen // 3
    step_z = chosen % 3 - 1
    tile_row = jnp.arange(TZ, dtype=jnp.int32)[:, None]
    return (groups * TZ + (tile_row + step_z) % TZ).astype(jnp.int32)


def set_ends(result, own_key, smallest, high):
    shape = result.shape
    spot = [jax.random.randint(jax.random.fold_in(own_key, axis), (), 0, shape[axis]) for axis in range(len(shape))]
    result = result.at[tuple(spot)].set(smallest)
    longest = shape.index(max(shape))
    spot[longest] = (spot[longest] + 1) % shape[longest]
    return result.at[tuple(spot)].set(high)


def shard_levels(key, dims, split, least, high):
    factor_of = 1.0
    for axis_at, shards_of in split:
        draws = jax.random.uniform(jax.random.fold_in(jax.random.fold_in(key, 6), axis_at), (shards_of,), jnp.float32, least / len(split), high / len(split))
        factor_of = factor_of * jnp.repeat(jnp.exp(draws), dims[axis_at] // shards_of).reshape((-1,) + (1,) * (len(dims) - 1 - axis_at))
    return factor_of


def bell_draw(stream_key, dims, deviation, most, shards=(), held_as=jnp.bfloat16):
    result = deviation * jax.random.normal(stream_key, dims, jnp.float32)
    if shards:
        result = result * shard_levels(stream_key, dims, shards, -0.22, 0.18)
    return jnp.clip(result, -most, most).astype(held_as)


def setup_inputs(seed: int = 0) -> dict:
    keys = jax.random.split(jax.random.key(seed), 6)
    positions = jnp.clip(1.0 * jax.random.uniform(keys[0], (GRID_X, GRID_Y, TZ, 3, 128), jnp.float32) ** shard_levels(keys[0], (GRID_X, GRID_Y, TZ, 3, 128), ((0, 48), (1, 16)), -0.2, 0.2), 0.0, 1.0)
    masses = jnp.clip(jnp.exp(math.log(2.0) - 2.3025851 * jax.random.uniform(keys[1], (GRID_X, GRID_Y, TZ, 128), jnp.float32) ** shard_levels(keys[1], (GRID_X, GRID_Y, TZ, 128), ((0, 48), (1, 16)), -0.2, 0.2)), 0.2, 2.0)
    velocities = bell_draw(keys[2], (GRID_X, GRID_Y, TZ, 3, 128), 1.0, 6.0, ((0, 48), (1, 16)), jnp.float32)
    tile_counts = set_ends(jax.random.randint(keys[3], (GRID_X, GRID_Y, TZ), 32, 129), jax.random.fold_in(keys[3], 1), 32, 128).astype(jnp.int32)
    neighbour_list = draw_neighbour_list(jax.random.fold_in(keys[5], 71), 0)
    return {"positions": positions, "masses": masses, "velocities": velocities, "tile_counts": tile_counts, "neighbour_list": neighbour_list}


smoothing = 0.1
screening = 0.01
split_scale = 2.0
softening = 0.05
long_kick = 1.0
short_kick = 0.05


def wave_terms(length, first_index, extent):
    wavenum = (first_index + jnp.arange(extent, dtype=jnp.int32)).astype(jnp.float32)
    angles = wavenum * (2.0 * jnp.pi / length)
    return 4.0 * jnp.sin(0.5 * angles) ** 2, jnp.sin(angles)


def cloud_stencil(positions, cells_x, cells_y, cells_z, tiles):
    span = cells_z // tiles
    tile_row = jnp.arange(tiles, dtype=jnp.int32)[:, None]
    coord_x = positions[..., 0, :] * cells_x - 0.5
    base_x = jnp.clip(jnp.floor(coord_x), 0, cells_x - 2)
    frac_x = jnp.clip(coord_x - base_x, 0.0, 1.0)
    coord_y = positions[..., 1, :] * cells_y - 0.5
    base_y = jnp.clip(jnp.floor(coord_y), 0, cells_y - 2)
    frac_y = jnp.clip(coord_y - base_y, 0.0, 1.0)
    coord_z = (tile_row + positions[..., 2, :]) * span - 0.5
    base_z = jnp.floor(coord_z)
    frac_z = coord_z - base_z
    index_x = base_x.astype(jnp.int32)
    index_y = base_y.astype(jnp.int32)
    index_z = base_z.astype(jnp.int32) % cells_z
    cell_list = []
    weight_list = []
    for offset_x in (0, 1):
        for offset_y in (0, 1):
            for offset_z in (0, 1):
                weight_x = frac_x if offset_x else 1.0 - frac_x
                weight_y = frac_y if offset_y else 1.0 - frac_y
                weight_z = frac_z if offset_z else 1.0 - frac_z
                cell_list.append((((index_x + offset_x) * cells_y + index_y + offset_y) * cells_z + (index_z + offset_z) % cells_z).astype(jnp.int32))
                weight_list.append(weight_x * weight_y * weight_z)
    return jnp.stack(cell_list, axis=-2), jnp.stack(weight_list, axis=-2)


def pair_accel(receivers, sources, shifts):
    parts = []
    for comp in range(3):
        parts.append(shifts[:, :, comp, None, None] + sources[:, :, comp, None, :] - receivers[:, None, comp, :, None])
    square = parts[0] * parts[0] + parts[1] * parts[1] + parts[2] * parts[2]
    strength = sources[:, :, 3, None, :] * jnp.exp(-square / split_scale) * (square + softening) ** -1.5
    return jnp.stack([jnp.sum(strength * parts[comp], axis=(1, 3)) for comp in range(3)], axis=1)


def reference(positions, masses, velocities, tile_counts, neighbour_list):
    slot_index = jnp.arange(128, dtype=jnp.int32)
    live_mask = (slot_index < tile_counts[..., None]).astype(jnp.float32)
    mass_live = masses * live_mask
    cell_index, cloud_weights = cloud_stencil(positions, CX, CY, NZ, TZ)
    row_index = jnp.arange(GRID_X, dtype=jnp.int32)[:, None, None, None, None]
    column_index = jnp.arange(GRID_Y, dtype=jnp.int32)[None, :, None, None, None]
    cell_x = row_index * CX + cell_index // (CY * NZ)
    cell_y = column_index * CY + (cell_index // NZ) % CY
    flat_cells = ((cell_x * NY + cell_y) * NZ + cell_index % NZ).astype(jnp.int32)
    amounts = cloud_weights * mass_live[:, :, :, None, :]
    density = jax.ops.segment_sum(amounts.reshape(-1), flat_cells.reshape(-1), num_segments=NX * NY * NZ).reshape(NX, NY, NZ)
    spectrum = jnp.fft.fftn(density)
    kappa_x, sine_x = wave_terms(NX, 0, NX)
    kappa_y, sine_y = wave_terms(NY, 0, NY)
    kappa_z, sine_z = wave_terms(NZ, 0, NZ)
    kappa_sum = kappa_x[:, None, None] + kappa_y[None, :, None] + kappa_z[None, None, :]
    potential = spectrum * (-jnp.exp(-smoothing * kappa_sum) / (kappa_sum + screening))
    sine_list = (sine_x[:, None, None], sine_y[None, :, None], sine_z[None, None, :])
    picked = []
    for sine_part in sine_list:
        force_field = jnp.real(jnp.fft.ifftn(-1j * sine_part * potential)).reshape(-1)
        picked.append(jnp.sum(cloud_weights * force_field[flat_cells], axis=3))
    long_accel = jnp.stack(picked, axis=3)
    packed = jnp.concatenate([positions, mass_live[:, :, :, None, :]], axis=3)
    shell = jnp.stack([jnp.roll(packed, (-step_x, -step_y), axis=(0, 1)) for step_x in (-1, 0, 1) for step_y in (-1, 0, 1)])
    groups = neighbour_list // TZ
    layers = neighbour_list % TZ
    rows_four = jnp.arange(GRID_X, dtype=jnp.int32)[:, None, None, None]
    columns_four = jnp.arange(GRID_Y, dtype=jnp.int32)[None, :, None, None]
    sources = shell[groups, rows_four, columns_four, layers]
    tile_row = jnp.arange(TZ, dtype=jnp.int32)[:, None]
    shifts = jnp.stack([groups // 3 - 1, groups % 3 - 1, (layers - tile_row + 1) % TZ - 1], axis=-1).astype(jnp.float32)
    tile_total = GRID_X * GRID_Y * TZ
    listed = neighbour_list.shape[-1]
    short_accel = lax.map(lambda pieces: pair_accel(*pieces), (positions.reshape(tile_total // 16, 16, 3, 128), sources.reshape(tile_total // 16, 16, listed, 4, 128), shifts.reshape(tile_total // 16, 16, listed, 3)))
    short_accel = short_accel.reshape(GRID_X, GRID_Y, TZ, 3, 128)
    return velocities + live_mask[:, :, :, None, :] * (long_kick * long_accel + short_kick * short_accel)
```

```python
import functools

import jax
import jax.numpy as jnp
import ml_dtypes
import numpy as np
from jax import lax
from jax.experimental import pallas as pl
from jax.experimental.pallas import tpu as pltpu
from jax.sharding import PartitionSpec as P

CX = 2
CY = 6
NZ = 1024
TZ = 16
NB = 6
NX = 96
NY = 96
PX = 48
PY = 16
CELLS = NZ // TZ
BLOCK = NZ // PY
HALF = BLOCK // 2

smoothing = 0.1
screening = 0.01
split_scale = 2.0
softening = 0.05
long_kick = 1.0
short_kick = 0.05

f32 = jnp.float32
bf16 = jnp.bfloat16


def halves(table):
    high = table.astype(np.float32).astype(ml_dtypes.bfloat16)
    low = (table - high.astype(np.float64)).astype(np.float32).astype(ml_dtypes.bfloat16)
    return high, low


def real_basis(length, run):
    cells = np.arange(length)[:, None]
    wave = np.arange(length // 2)
    angle = 2 * np.pi * (cells * wave[None] % length) / length
    cosine = np.cos(angle) * np.sqrt(2 / length)
    sine = np.sin(angle) * np.sqrt(2 / length)
    step = np.sin(2 * np.pi * wave / length)
    cos_slope = sine * step
    sin_slope = -cosine * step
    cosine[:, 0] = np.sqrt(1 / length)
    sine[:, 0] = np.where(cells[:, 0] % 2 == 0, 1.0, -1.0) * np.sqrt(1 / length)
    cos_slope[:, 0] = 0
    sin_slope[:, 0] = 0
    kappa_cos = 4 * np.sin(np.pi * wave / length) ** 2
    kappa_sin = kappa_cos.copy()
    kappa_sin[0] = 4.0

    def laid(first, second):
        shape = first.shape[:-1] + (-1, 1, run)
        return np.concatenate([first.reshape(shape), second.reshape(shape)], axis=-2).reshape(
            first.shape[:-1] + (length,)
        )

    return (
        laid(cosine, sine),
        laid(cos_slope, sin_slope),
        laid(kappa_cos, kappa_sin),
        laid(-step, step),
    )


@functools.lru_cache(None)
def tables():
    basis_z, _, kappa_z, sine_z = real_basis(NZ, HALF)
    basis_x, slope_x, kappa_x, _ = real_basis(NX, 1)
    basis_y, slope_y, kappa_y, _ = real_basis(NY, 1)
    out = {}
    out["fwd_z"] = halves(basis_z)
    out["inv_z"] = halves(basis_z.T)
    pad_y = np.zeros((NY, PY, 8))
    pad_y[:, :, :CY] = basis_y.T.reshape(NY, PY, CY)
    out["fwd_y"] = halves(pad_y.reshape(NY, PY * 8))
    out["fwd_x"] = halves(basis_x.reshape(PX, CX, NX).transpose(2, 1, 0).reshape(NX, CX * PX))
    both = np.stack([slope_x.reshape(PX, CX, NX), basis_x.reshape(PX, CX, NX)], axis=1)
    out["inv_x"] = halves(both.reshape(PX * 2 * CX, NX))

    def rows_y(table):
        padded = np.zeros((2, PY, 8, PX))
        padded[:, :, :CY] = table.reshape(PY, CY, PX, 2).transpose(3, 0, 1, 2)
        return padded.reshape(2 * PY * 8, PX)

    out["inv_y"] = halves(np.concatenate([rows_y(basis_y), rows_y(slope_y)], axis=0))
    out["kappa_x"] = kappa_x[:, None].astype(np.float32)
    out["kappa_y"] = np.repeat(kappa_y.reshape(PX, 2), BLOCK, axis=1).astype(np.float32)
    out["kappa_z"] = np.tile(kappa_z.reshape(PY, BLOCK), (1, 2)).astype(np.float32)
    out["sine_z"] = np.tile(sine_z.reshape(PY, BLOCK), (1, 2)).astype(np.float32)
    return out


def split(value):
    high = value.astype(bf16)
    return high, (value - high.astype(f32)).astype(bf16)


def dot(left, right):
    return lax.dot_general(left, right, (((1,), (0,)), ((), ())), preferred_element_type=f32)


def dot_t(left, right):
    return lax.dot_general(left, right, (((1,), (1,)), ((), ())), preferred_element_type=f32)


def table_dot(high_ref, low_ref, value):
    high, low = split(value)
    return dot(high_ref[...], high) + dot(high_ref[...], low) + dot(low_ref[...], high)


def dot_table(value, high_ref, low_ref):
    rows = value.shape[0]
    high, low = split(value)
    both = dot(jnp.concatenate([high, low], axis=0), high_ref[...])
    return both[:rows] + both[rows:] + dot(high, low_ref[...])


def iota(shape, dim):
    return lax.broadcasted_iota(jnp.int32, shape, dim)


def plane_weights(pos_ref, tile):
    row = iota((16, 128), 0)
    row_x = (row >> 3).astype(f32)
    row_y = (row & 7).astype(f32)
    x = jnp.clip(pos_ref[0, tile : tile + 1, :] * CX - 0.5, 0.0, 1.0)
    y = jnp.clip(pos_ref[1, tile : tile + 1, :] * CY - 0.5, 0.0, CY - 1.0)
    return (1.0 - jnp.abs(x - row_x)) * jnp.maximum(1.0 - jnp.abs(y - row_y), 0.0)


def depth_weights(pos_ref, tile):
    z = (tile + pos_ref[2, tile : tile + 1, :]) * CELLS - 0.5 - (tile * CELLS - CELLS // 2)
    return jnp.maximum(1.0 - jnp.abs(z - iota((128, 128), 0).astype(f32)), 0.0)


def deposit_kernel(counts, pos_ref, mass_ref, high_ref, low_ref, out_ref):
    slot = iota((1, 128), 1)
    windows = []
    for tile in range(TZ):
        mass = jnp.where(slot < counts[0, tile], mass_ref[tile : tile + 1, :], 0.0)
        flat_high, flat_low = split(plane_weights(pos_ref, tile) * mass)
        deep_high, deep_low = split(depth_weights(pos_ref, tile))
        windows.append(
            dot_t(flat_high, deep_high) + dot_t(flat_high, deep_low) + dot_t(flat_low, deep_high)
        )
    even = jnp.concatenate(windows[0::2], axis=1)
    odd = jnp.concatenate(windows[1::2], axis=1)
    density = pltpu.roll(even, NZ - CELLS // 2, 1) + pltpu.roll(odd, CELLS // 2, 1)
    modes = dot_table(density, high_ref, low_ref)
    first = iota((8, 128), 1) < BLOCK
    for pair in range(PY // 2):
        lanes = slice(128 * pair, 128 * (pair + 1))
        near = modes[:8, lanes]
        far = modes[8:, lanes]
        out_ref[2 * pair] = jnp.where(first, near, pltpu.roll(far, BLOCK, 1))
        out_ref[2 * pair + 1] = jnp.where(first, pltpu.roll(near, BLOCK, 1), far)


def forward_y_kernel(in_ref, high_ref, low_ref, out_ref):
    out_ref[...] = table_dot(high_ref, low_ref, in_ref[...])


def solve_x_kernel(
    in_ref, fwd_high, fwd_low, inv_high, inv_low, kappa_x, kappa_y, kappa_z, out_ref
):
    at_x = lax.axis_index(("gx", "gz"))
    at_y = lax.axis_index("gy")
    first = iota((PX, 128), 1) < BLOCK
    wave_a = in_ref[pl.ds(0, PX, stride=2), :]
    wave_b = in_ref[pl.ds(1, PX, stride=2), :]
    cells_0 = jnp.where(first, wave_a, pltpu.roll(wave_b, BLOCK, 1))
    cells_1 = jnp.where(first, pltpu.roll(wave_a, BLOCK, 1), wave_b)
    spectrum = table_dot(fwd_high, fwd_low, jnp.concatenate([cells_0, cells_1], axis=0))
    kappa_sum = kappa_x[...] + (kappa_y[pl.ds(at_x, 1), :] + kappa_z[pl.ds(at_y, 1), :])
    potential = spectrum * (-jnp.exp(-smoothing * kappa_sum) / (kappa_sum + screening))
    out_ref[...] = table_dot(inv_high, inv_low, potential)


def inverse_y_kernel(in_ref, high_ref, low_ref, out_ref):
    rows = PY * 8
    first = iota((rows, 128), 1) < BLOCK
    fields = [in_ref[pl.ds(at, PX, stride=4), :] for at in range(4)]
    slope_x_high, slope_x_low = split(jnp.concatenate(fields[:2], axis=1))
    phi_high, phi_low = split(jnp.concatenate(fields[2:], axis=1))

    def product(table_rows, high, low):
        a = high_ref[table_rows, :]
        return dot(a, high) + dot(a, low) + dot(low_ref[table_rows, :], high)

    force_x = product(slice(0, 2 * rows), slope_x_high, slope_x_low)
    others = product(slice(0, 4 * rows), phi_high, phi_low)
    for field, value in enumerate((force_x, others[2 * rows :], others[: 2 * rows])):
        cos_0, cos_1 = value[:rows, :128], value[:rows, 128:]
        sin_0, sin_1 = value[rows:, :128], value[rows:, 128:]
        cell_0 = cos_0 + pltpu.roll(sin_0, BLOCK, 1)
        cell_1 = pltpu.roll(cos_1, BLOCK, 1) + sin_1
        merged = jnp.where(first, cell_0, cell_1)
        out_ref[:, 8 * field : 8 * field + 8, :] = merged.reshape(PY, 8, 128)


def kick_kernel(
    counts, in_ref, pos_ref, vel_ref, short_ref, high_ref, low_ref, sine_ref, out_ref
):
    first = iota((24, 128), 1) < BLOCK
    cosines = (iota((8, 128), 1) & (BLOCK - 1)) < HALF
    slot = iota((1, 128), 1)

    def block(at):
        value = in_ref[at]
        phi = value[16:24]
        turned = jnp.where(
            cosines, pltpu.roll(phi, 128 - HALF, 1), pltpu.roll(phi, HALF, 1)
        )
        return jnp.concatenate([value[:16], turned * sine_ref[at : at + 1, :]], axis=0)

    near, far = [], []
    for pair in range(PY // 2):
        a, b = block(2 * pair), block(2 * pair + 1)
        near.append(jnp.where(first, a, pltpu.roll(b, BLOCK, 1)))
        far.append(jnp.where(first, pltpu.roll(a, BLOCK, 1), b))
    modes = jnp.concatenate(
        [jnp.concatenate(near, axis=1), jnp.concatenate(far, axis=1)], axis=0
    )
    forces = dot_table(modes, high_ref, low_ref)
    shifted = (
        pltpu.roll(forces, CELLS // 2, 1),
        pltpu.roll(forces, NZ - CELLS // 2, 1),
    )
    for tile in range(TZ):
        start = 128 * (tile // 2)
        window = shifted[tile % 2][:, start : start + 128]
        high, low = split(window)
        deep_high, deep_low = split(depth_weights(pos_ref, tile))
        both = dot(jnp.concatenate([high, low], axis=0), deep_high)
        picked = both[:48] + both[48:] + dot(high, deep_low)
        flat = plane_weights(pos_ref, tile)
        live = slot < counts[0, tile]
        for comp in range(3):
            at = 8 * comp
            total = flat[:8] * picked[at : at + 8] + flat[8:] * picked[24 + at : 32 + at]
            long_accel = jnp.sum(total, axis=0, keepdims=True)
            kick = long_kick * long_accel + short_kick * short_ref[comp, tile : tile + 1, :]
            out_ref[comp, tile : tile + 1, :] = vel_ref[comp, tile : tile + 1, :] + jnp.where(
                live, kick, 0.0
            )


def short_kernel(listed, own_ref, left_ref, mid_ref, right_ref, out_ref, shell, sums):
    for at, ref in enumerate((left_ref, mid_ref, right_ref)):
        for dx in range(3):
            shell[3 * dx + at] = ref[dx]

    def one_tile(tile, carry):
        rows = [own_ref[comp, pl.ds(tile, 1), :] for comp in range(3)]
        columns = jnp.concatenate(rows + [jnp.zeros((5, 128), f32)], axis=0).T
        sources = []
        for entry in range(NB):
            code = listed[entry, tile]
            group = code >> 4
            layer = code & (TZ - 1)
            step_x = (group * 11) >> 5
            step_y = group - 3 * step_x
            step_z = (layer - tile + 1) & (TZ - 1)
            shifts = [(step - 1).astype(f32) for step in (step_x, step_y, step_z)]
            source = [shell[group, comp, pl.ds(layer, 1), :] for comp in range(4)]
            sources.append([source[comp] + shifts[comp] for comp in range(3)] + [source[3]])
        for chunk in range(16):
            part = slice(8 * chunk, 8 * chunk + 8)
            own = [jnp.broadcast_to(columns[part, comp : comp + 1], (8, 128)) for comp in range(3)]
            totals = [None] * 3
            for x, y, z, mass in sources:
                apart = [x - own[0], y - own[1], z - own[2]]
                square = apart[0] * apart[0] + apart[1] * apart[1] + apart[2] * apart[2]
                root = lax.rsqrt(square + softening)
                strength = (mass * jnp.exp(square * (-1.0 / split_scale))) * (root * root * root)
                for comp in range(3):
                    term = strength * apart[comp]
                    totals[comp] = term if totals[comp] is None else totals[comp] + term
            for comp in range(3):
                sums[128 * comp + 8 * chunk : 128 * comp + 8 * chunk + 8, :] = totals[comp]
        ones = jnp.ones((8, 128), bf16)
        high, low = split(sums[...])
        total = dot_t(ones, high) + dot_t(ones, low)
        for comp in range(3):
            out_ref[comp, pl.ds(tile, 1), :] = total[:1, 128 * comp : 128 * comp + 128]
        return carry

    lax.fori_loop(0, TZ, one_tile, 0)


def call(kernel, shape, operands, smem=0, scratch=(), cost=None):
    specs = [pl.BlockSpec(memory_space=pltpu.SMEM)] * smem
    specs += [pl.BlockSpec(memory_space=pltpu.VMEM)] * (len(operands) - smem)
    return pl.pallas_call(
        kernel,
        out_shape=jax.ShapeDtypeStruct(shape, f32),
        in_specs=specs,
        out_specs=pl.BlockSpec(memory_space=pltpu.VMEM),
        scratch_shapes=scratch,
        cost_estimate=cost,
        compiler_params=pltpu.CompilerParams(vmem_limit_bytes=24 << 20),
    )(*operands)


def exchange(value, axis):
    return lax.all_to_all(value, axis, split_axis=0, concat_axis=0, tiled=True)


def shift(value, axis, count, step):
    return lax.ppermute(value, axis, [(i, (i + step) % count) for i in range(count)])


def shards(positions, masses, velocities, tile_counts, neighbour_list):
    t = tables()
    wide = ("gx", "gz")
    position = jnp.transpose(positions[0, 0], (1, 0, 2))
    velocity = jnp.transpose(velocities[0, 0], (1, 0, 2))
    mass = masses[0, 0]
    counts = tile_counts[0]
    listed = jnp.transpose(neighbour_list[0, 0], (1, 0))

    modes = call(deposit_kernel, (PY, 8, 128), (counts, position, mass, *t["fwd_z"]), smem=1)

    live = lax.broadcasted_iota(jnp.int32, (TZ, 128), 1) < counts[0][:, None]
    packed = jnp.concatenate([position, jnp.where(live, mass, 0.0)[None]], axis=0)
    row = jnp.stack([shift(packed, wide, PX, 1), packed, shift(packed, wide, PX, -1)])
    left = shift(row, "gy", PY, 1)
    right = shift(row, "gy", PY, -1)

    modes = exchange(modes, "gy").reshape(PY * 8, 128)
    modes = call(forward_y_kernel, (NY, 128), (modes, *t["fwd_y"]))
    modes = exchange(modes.reshape(PX, 2, 128), wide).reshape(NY, 128)
    modes = call(
        solve_x_kernel,
        (4 * PX, 128),
        (modes, *t["fwd_x"], *t["inv_x"], t["kappa_x"], t["kappa_y"], t["kappa_z"]),
    )
    fields = exchange(modes.reshape(PX, 4, 128), wide).reshape(4 * PX, 128)
    short = call(
        short_kernel,
        (3, TZ, 128),
        (listed, position, left, row, right),
        smem=1,
        scratch=[pltpu.VMEM((9, 4, TZ, 128), f32), pltpu.VMEM((3 * 128, 128), f32)],
        cost=pl.CostEstimate(
            flops=22 * TZ * NB * 128 * 128,
            bytes_accessed=400_000,
            transcendentals=2 * TZ * NB * 128 * 128,
        ),
    )
    fields = call(inverse_y_kernel, (PY, 24, 128), (fields, *t["inv_y"]))
    fields = exchange(fields, "gy")
    kicked = call(
        kick_kernel,
        (3, TZ, 128),
        (counts, fields, position, velocity, short, *t["inv_z"], t["sine_z"]),
        smem=1,
    )
    return jnp.transpose(kicked, (1, 0, 2))[None, None]


def solution(mesh):
    wide = ("gx", "gz")
    placed = (
        P(wide, "gy", None, None, None),
        P(wide, "gy", None, None),
        P(wide, "gy", None, None, None),
        P(wide, "gy", None),
        P(wide, "gy", None, None),
    )
    return jax.shard_map(
        shards,
        mesh=mesh,
        in_specs=placed,
        out_specs=P(wide, "gy", None, None, None),
        check_vma=False,
    )
```

```python
import functools

import jax
import jax.numpy as jnp
import ml_dtypes
import numpy as np
from jax import lax
from jax.experimental import pallas as pl
from jax.experimental.pallas import tpu as pltpu
from jax.sharding import PartitionSpec as P

CX = 2
CY = 6
NZ = 1024
TZ = 16
NB = 6
NX = 96
NY = 96
PX = 48
PY = 16
CELLS = NZ // TZ
BLOCK = NZ // PY
HALF = BLOCK // 2
PIECES = 4 * TZ // 2

smoothing = 0.1
screening = 0.01
split_scale = 2.0
softening = 0.05
long_kick = 1.0
short_kick = 0.05

f32 = jnp.float32
bf16 = jnp.bfloat16


def halves(table):
    high = table.astype(np.float32).astype(ml_dtypes.bfloat16)
    low = (table - high.astype(np.float64)).astype(np.float32).astype(ml_dtypes.bfloat16)
    return high, low


def real_basis(length, run):
    cells = np.arange(length)[:, None]
    wave = np.arange(length // 2)
    angle = 2 * np.pi * (cells * wave[None] % length) / length
    cosine = np.cos(angle) * np.sqrt(2 / length)
    sine = np.sin(angle) * np.sqrt(2 / length)
    step = np.sin(2 * np.pi * wave / length)
    cos_slope = sine * step
    sin_slope = -cosine * step
    cosine[:, 0] = np.sqrt(1 / length)
    sine[:, 0] = np.where(cells[:, 0] % 2 == 0, 1.0, -1.0) * np.sqrt(1 / length)
    cos_slope[:, 0] = 0
    sin_slope[:, 0] = 0
    kappa_cos = 4 * np.sin(np.pi * wave / length) ** 2
    kappa_sin = kappa_cos.copy()
    kappa_sin[0] = 4.0

    def laid(first, second):
        shape = first.shape[:-1] + (-1, 1, run)
        return np.concatenate([first.reshape(shape), second.reshape(shape)], axis=-2).reshape(
            first.shape[:-1] + (length,)
        )

    return (
        laid(cosine, sine),
        laid(cos_slope, sin_slope),
        laid(kappa_cos, kappa_sin),
        laid(-step, step),
    )


def depth_basis():
    table = np.zeros((4, 2, 128, 256))
    waves = np.zeros((4, 128))
    waves[0] = np.concatenate([8 * np.arange(64), 8 * np.arange(64) + 4])
    for residue in (1, 2, 3):
        waves[residue] = 8 * np.arange(128) + residue
    angle = 2 * np.pi * (np.arange(128)[:, None] * waves[:, None] % NZ) / NZ
    cosine = np.cos(angle) * np.sqrt(2 / NZ)
    sine = np.sin(angle) * np.sqrt(2 / NZ)
    cosine[0, :, 0] = np.sqrt(1 / NZ)
    sine[0, :, 0] = np.where(np.arange(128) % 2 == 0, 1.0, -1.0) * np.sqrt(1 / NZ)
    step = np.sin(2 * np.pi * waves / NZ)
    kappa_cos = 4 * np.sin(np.pi * waves / NZ) ** 2
    kappa_sin = kappa_cos.copy()
    step[0, 0] = 0
    kappa_sin[0, 0] = 4.0

    def laid(first, second):
        shape = first.shape[:-1] + (4, 1, HALF)
        return np.concatenate([first.reshape(shape), second.reshape(shape)], axis=-2).reshape(
            first.shape[:-1] + (256,)
        )

    table[:, 0] = laid(cosine, sine)
    table[:, 1] = laid(-sine, cosine)
    table[0, 1, :, 128:] = table[0, 0, :, 128:]
    table[0, 0, :, 128:] = 0
    table[0, 1, :, :128] = 0
    return (
        table.reshape(4, 256, 256),
        laid(kappa_cos, kappa_sin).reshape(NZ),
        laid(-step, step).reshape(NZ),
    )


ROOT_HALF = float(np.sqrt(0.5))


def waves_of(cells):
    total = [cells[a] + cells[a + 4] for a in range(4)]
    apart = [cells[a] - cells[a + 4] for a in range(4)]
    even, odd = total[0] + total[2], total[1] + total[3]
    less, more = (apart[1] - apart[3]) * ROOT_HALF, (apart[1] + apart[3]) * ROOT_HALF
    pairs = (
        (even + odd, even - odd),
        (apart[0] + less, more + apart[2]),
        (total[0] - total[2], total[1] - total[3]),
        (apart[0] - less, more - apart[2]),
    )
    return [jnp.concatenate(pair, axis=1) for pair in pairs]


def cells_of(pairs):
    (zero, four), one, two, three = [(pair[:, :128], pair[:, 128:]) for pair in pairs]
    plus, minus = zero + four, zero - four
    even = (plus + two[0], minus + two[1], plus - two[0], minus - two[1])
    less, more = (one[0] - three[0]) * ROOT_HALF, (one[1] + three[1]) * ROOT_HALF
    odd = (one[0] + three[0], more + less, one[1] - three[1], more - less)
    return [even[a] + odd[a] for a in range(4)] + [even[a] - odd[a] for a in range(4)]


@functools.lru_cache(None)
def tables():
    table_z, kappa_z, sine_z = depth_basis()
    basis_x, slope_x, kappa_x, _ = real_basis(NX, 1)
    basis_y, slope_y, kappa_y, _ = real_basis(NY, 1)
    out = {}
    out["fwd_z"] = np.concatenate(halves(table_z), axis=0)
    out["inv_z"] = np.concatenate(halves(table_z.transpose(0, 2, 1)), axis=0)
    pad_y = np.zeros((2, PX, PY, 8))
    pad_y[..., :CY] = basis_y.T.reshape(PX, 2, PY, CY).transpose(1, 0, 2, 3)
    out["fwd_y"] = halves(pad_y.reshape(NY, PY * 8))
    out["fwd_x"] = halves(basis_x.reshape(PX, CX, NX).transpose(2, 1, 0).reshape(NX, CX * PX))
    both = np.stack([slope_x.reshape(PX, CX, NX), basis_x.reshape(PX, CX, NX)])
    out["inv_x"] = halves(both.transpose(0, 2, 1, 3).reshape(2 * CX * PX, NX))

    rows = np.zeros((2, PY, 3, CY, 2, PX))
    spread = [table.reshape(PY, CY, PX, 2).transpose(3, 0, 1, 2) for table in (basis_y, slope_y)]
    rows[:, :, 0, :, 0] = spread[0]
    rows[:, :, 1, :, 1] = spread[1]
    rows[:, :, 2, :, 1] = spread[0]
    out["inv_y"] = halves(rows.reshape(2 * PY * 3 * CY, 2 * PX))
    out["kappa_x"] = kappa_x[:, None].astype(np.float32)
    out["kappa_y"] = np.repeat(kappa_y.reshape(PX, 2), BLOCK, axis=1).astype(np.float32)
    out["kappa_z"] = np.tile(kappa_z.reshape(PY, BLOCK), (1, 2)).astype(np.float32)
    out["sine_z"] = np.tile(sine_z.reshape(PY, BLOCK), (1, 2)).astype(np.float32)
    return out


def split(value):
    high = value.astype(bf16)
    return high, (value - high.astype(f32)).astype(bf16)


def dot(left, right):
    return lax.dot_general(left, right, (((1,), (0,)), ((), ())), preferred_element_type=f32)


def dot_t(left, right):
    return lax.dot_general(left, right, (((1,), (1,)), ((), ())), preferred_element_type=f32)


def table_dot(high_ref, low_ref, value):
    high, low = split(value)
    return dot(high_ref[...], high) + dot(high_ref[...], low) + dot(low_ref[...], high)


def dot_table(value, table_ref, at):
    rows = value.shape[0]
    high, low = split(value)
    both = dot(jnp.concatenate([high, low], axis=0), table_ref[at])
    return both[:rows] + both[rows:] + dot(high, table_ref[4 + at])


def iota(shape, dim):
    return lax.broadcasted_iota(jnp.int32, shape, dim)


def plane_weights(pos_ref, tile):
    row = iota((16, 128), 0)
    row_x = (row >> 3).astype(f32)
    row_y = (row & 7).astype(f32)
    x = jnp.clip(pos_ref[0, tile : tile + 1, :] * CX - 0.5, 0.0, 1.0)
    y = jnp.clip(pos_ref[1, tile : tile + 1, :] * CY - 0.5, 0.0, CY - 1.0)
    return (1.0 - jnp.abs(x - row_x)) * jnp.maximum(1.0 - jnp.abs(y - row_y), 0.0)


def depth_weights(pos_ref, tile):
    z = (tile + pos_ref[2, tile : tile + 1, :]) * CELLS - 0.5 - (tile * CELLS - CELLS // 2)
    return jnp.maximum(1.0 - jnp.abs(z - iota((128, 128), 0).astype(f32)), 0.0)


def deposit_kernel(
    counts_hbm,
    pos_hbm,
    mass_hbm,
    table_hbm,
    out_ref,
    packed_ref,
    live_ref,
    counts,
    pos_ref,
    mass_ref,
    table_ref,
    arrived,
):
    loads = [
        pltpu.make_async_copy(source, held, arrived.at[at])
        for at, (source, held) in enumerate(
            (
                (counts_hbm, counts),
                (pos_hbm, pos_ref),
                (mass_hbm, mass_ref),
                (table_hbm, table_ref),
            )
        )
    ]
    for load in loads:
        load.start()
    for load in loads[:3]:
        load.wait()
    packed_ref[:3] = pos_ref[...]
    slot = iota((1, 128), 1)
    windows = []
    for tile in range(TZ):
        live = slot < counts[0, tile]
        live_ref[tile : tile + 1, :] = jnp.where(live, 1.0, 0.0)
        mass = jnp.where(live, mass_ref[tile : tile + 1, :], 0.0)
        packed_ref[3, tile : tile + 1, :] = mass
        flat_high, flat_low = split(plane_weights(pos_ref, tile) * mass)
        deep_high, deep_low = split(depth_weights(pos_ref, tile))
        windows.append(
            dot_t(flat_high, deep_high) + dot_t(flat_high, deep_low) + dot_t(flat_low, deep_high)
        )
    even = jnp.concatenate(windows[0::2], axis=1)
    odd = jnp.concatenate(windows[1::2], axis=1)
    density = pltpu.roll(even, NZ - CELLS // 2, 1) + pltpu.roll(odd, CELLS // 2, 1)
    pairs = waves_of([density[:, 128 * a : 128 * a + 128] for a in range(8)])
    loads[3].wait()
    modes = [dot_table(value, table_ref, at) for at, value in enumerate(pairs)]
    first = iota((8, 128), 1) < BLOCK
    for pair in range(PY // 2):
        part = modes[pair // 2][:, 128 * (pair % 2) : 128 * (pair % 2) + 128]
        near = part[:8]
        far = part[8:]
        out_ref[2 * pair] = jnp.where(first, near, pltpu.roll(far, BLOCK, 1))
        out_ref[2 * pair + 1] = jnp.where(first, pltpu.roll(near, BLOCK, 1), far)


def forward_y_kernel(in_ref, high_ref, low_ref, packed_ref, out_ref):
    value = table_dot(high_ref, low_ref, in_ref[...])
    for at in range(2):
        out_ref[pl.ds(at, PX, stride=4), :] = value[PX * at : PX * (at + 1)]
        out_ref[pl.ds(2 + at, PIECES, stride=4), :] = packed_ref[pl.ds(at, PIECES, stride=2), :]
        out_ref[pl.ds(4 * PIECES + 2 + at, PX - PIECES, stride=4), :] = jnp.zeros(
            (PX - PIECES, 128), f32
        )


def solve_x_kernel(
    in_ref, fwd_high, fwd_low, inv_high, inv_low, kappa_x, kappa_y, kappa_z, out_ref
):
    at_x = lax.axis_index(("gx", "gz"))
    at_y = lax.axis_index("gy")
    first = iota((PX, 128), 1) < BLOCK
    wave_a = in_ref[pl.ds(0, PX, stride=4), :]
    wave_b = in_ref[pl.ds(1, PX, stride=4), :]
    cells_0 = jnp.where(first, wave_a, pltpu.roll(wave_b, BLOCK, 1))
    cells_1 = jnp.where(first, pltpu.roll(wave_a, BLOCK, 1), wave_b)
    spectrum = table_dot(fwd_high, fwd_low, jnp.concatenate([cells_0, cells_1], axis=0))
    kappa_sum = kappa_x[...] + (kappa_y[pl.ds(at_x, 1), :] + kappa_z[pl.ds(at_y, 1), :])
    potential = spectrum * (-jnp.exp(-smoothing * kappa_sum) / (kappa_sum + screening))
    fields = table_dot(inv_high, inv_low, potential)
    for at in range(4):
        out_ref[pl.ds(at, PX, stride=8), :] = fields[PX * at : PX * (at + 1)]
    for at in range(2):
        piece = in_ref[pl.ds(2 + at, PX, stride=4), :]
        out_ref[pl.ds(4 + at, PX, stride=8), :] = pltpu.roll(piece, 1, 0)
        out_ref[pl.ds(6 + at, PX, stride=8), :] = pltpu.roll(piece, PX - 1, 0)


def inverse_y_kernel(in_ref, high_ref, low_ref, packed_ref, out_ref, row_ref):
    rows = PY * 3 * CY
    first = iota((rows, 128), 1) < BLOCK
    cells = [
        jnp.concatenate([in_ref[pl.ds(at, PX, stride=8), :] for at in (x, x + 2)], axis=0)
        for x in range(CX)
    ]
    value = table_dot(high_ref, low_ref, jnp.concatenate(cells, axis=1))
    cos_0, cos_1 = value[:rows, :128], value[:rows, 128:]
    sin_0, sin_1 = value[rows:, :128], value[rows:, 128:]
    cell_0 = cos_0 + pltpu.roll(sin_0, BLOCK, 1)
    cell_1 = pltpu.roll(cos_1, BLOCK, 1) + sin_1
    out_ref[...] = jnp.where(first, cell_0, cell_1)
    row_ref[1] = packed_ref[...]
    for at in range(2):
        for side in range(2):
            row_ref[2 * side, pl.ds(at, PIECES, stride=2), :] = in_ref[
                pl.ds(4 + 2 * side + at, PIECES, stride=8), :
            ]


def kick_kernel(
    live_ref, in_ref, pos_ref, vel_ref, short_ref, table_ref, sine_ref, out_ref
):
    first = iota((24, 128), 1) < BLOCK
    cosines = (iota((8, 128), 1) & (BLOCK - 1)) < HALF

    def block(at):
        last = PY * 3 * CY - 8
        parts = []
        for row in range(3 * CY * at, 3 * CY * (at + 1), CY):
            part = in_ref[min(row, last) : min(row, last) + 8, :]
            parts.append(part if row <= last else pltpu.roll(part, 8 - (row - last), 0))
        turned = jnp.where(
            cosines, pltpu.roll(parts[2], 128 - HALF, 1), pltpu.roll(parts[2], HALF, 1)
        )
        return jnp.concatenate(parts[:2] + [turned * sine_ref[at : at + 1, :]], axis=0)

    near, far = [], []
    for pair in range(PY // 2):
        a, b = block(2 * pair), block(2 * pair + 1)
        near.append(jnp.where(first, a, pltpu.roll(b, BLOCK, 1)))
        far.append(jnp.where(first, pltpu.roll(a, BLOCK, 1), b))
    modes = [jnp.concatenate(parts, axis=0) for parts in zip(near, far)]
    pairs = [
        dot_table(jnp.concatenate(modes[2 * at : 2 * at + 2], axis=1), table_ref, at)
        for at in range(4)
    ]
    forces = jnp.concatenate(cells_of(pairs), axis=1)
    shifted = (
        pltpu.roll(forces, CELLS // 2, 1),
        pltpu.roll(forces, NZ - CELLS // 2, 1),
    )
    for tile in range(TZ):
        start = 128 * (tile // 2)
        window = shifted[tile % 2][:, start : start + 128]
        high, low = split(window)
        deep_high, deep_low = split(depth_weights(pos_ref, tile))
        both = dot(jnp.concatenate([high, low], axis=0), deep_high)
        picked = both[:48] + both[48:] + dot(high, deep_low)
        flat = plane_weights(pos_ref, tile)
        live = live_ref[tile : tile + 1, :]
        for comp in range(3):
            at = 8 * comp
            total = flat[:8] * picked[at : at + 8] + flat[8:] * picked[24 + at : 32 + at]
            long_accel = jnp.sum(total, axis=0, keepdims=True)
            kick = long_kick * long_accel + short_kick * short_ref[comp, tile : tile + 1, :]
            out_ref[comp, tile : tile + 1, :] = vel_ref[comp, tile : tile + 1, :] + live * kick


def short_kernel(listed, left_ref, mid_ref, right_ref, out_ref, shell, sums_even, sums_odd):
    for at, ref in enumerate((left_ref, mid_ref, right_ref)):
        for dx in range(3):
            shell[3 * dx + at] = ref[dx]

    def pairs(tile, sums):
        rows = [shell[4, comp, pl.ds(tile, 1), :] for comp in range(3)]
        columns = jnp.concatenate(rows + [jnp.zeros((5, 128), f32)], axis=0).T
        sources = []
        for entry in range(NB):
            code = listed[entry, tile]
            group = code >> 4
            layer = code & (TZ - 1)
            step_x = (group * 11) >> 5
            step_y = group - 3 * step_x
            step_z = (layer - tile + 1) & (TZ - 1)
            shifts = [(step - 1).astype(f32) for step in (step_x, step_y, step_z)]
            source = [shell[group, comp, pl.ds(layer, 1), :] for comp in range(4)]
            sources.append([source[comp] + shifts[comp] for comp in range(3)] + [source[3]])
        for chunk in range(16):
            part = slice(8 * chunk, 8 * chunk + 8)
            own = [jnp.broadcast_to(columns[part, comp : comp + 1], (8, 128)) for comp in range(3)]
            totals = [None] * 3
            for x, y, z, mass in sources:
                apart = [x - own[0], y - own[1], z - own[2]]
                square = apart[0] * apart[0] + apart[1] * apart[1] + apart[2] * apart[2]
                root = lax.rsqrt(square + softening)
                strength = (mass * jnp.exp(square * (-1.0 / split_scale))) * (root * root * root)
                for comp in range(3):
                    term = strength * apart[comp]
                    totals[comp] = term if totals[comp] is None else totals[comp] + term
            for comp in range(3):
                sums[128 * comp + 8 * chunk : 128 * comp + 8 * chunk + 8, :] = totals[comp]

    def add_up(tile, sums):
        ones = jnp.ones((8, 128), bf16)
        high, low = split(sums[...])
        total = dot_t(ones, high) + dot_t(ones, low)
        for comp in range(3):
            out_ref[comp, pl.ds(tile, 1), :] = total[:1, 128 * comp : 128 * comp + 128]

    def two(at, carry):
        add_up(2 * at, sums_even)
        pairs(2 * at + 1, sums_odd)
        add_up(2 * at + 1, sums_odd)
        pairs(2 * at + 2, sums_even)
        return carry

    pairs(0, sums_even)
    lax.fori_loop(0, TZ // 2 - 1, two, 0)
    add_up(TZ - 2, sums_even)
    pairs(TZ - 1, sums_odd)
    add_up(TZ - 1, sums_odd)


def call(kernel, shapes, operands, spaces="", scratch=(), cost=None, room=24 << 20):
    space_of = {"s": pltpu.SMEM, "h": pltpu.HBM, "a": pl.ANY, "v": pltpu.VMEM}
    spaces = spaces.ljust(len(operands), "v")
    return pl.pallas_call(
        kernel,
        out_shape=[jax.ShapeDtypeStruct(shape, f32) for shape in shapes],
        in_specs=[pl.BlockSpec(memory_space=space_of[space]) for space in spaces],
        out_specs=[pl.BlockSpec(memory_space=pltpu.VMEM)] * len(shapes),
        scratch_shapes=scratch,
        cost_estimate=cost,
        compiler_params=pltpu.CompilerParams(vmem_limit_bytes=room),
    )(*operands)


def exchange(value, axis):
    return lax.all_to_all(value, axis, split_axis=0, concat_axis=0, tiled=True)


def shift(value, axis, count, step):
    return lax.ppermute(value, axis, [(i, (i + step) % count) for i in range(count)])


def short_range(*operands):
    pairs = TZ * NB * 128 * 128
    (short,) = call(
        short_kernel,
        [(3, TZ, 128)],
        operands,
        spaces="s",
        scratch=[pltpu.VMEM((9, 4, TZ, 128), f32)] + [pltpu.VMEM((3 * 128, 128), f32)] * 2,
        cost=pl.CostEstimate(flops=40_000 * pairs, bytes_accessed=400_000, transcendentals=2 * pairs),
    )
    return short


def shards(positions, masses, velocities, tile_counts, neighbour_list):
    t = tables()
    wide = ("gx", "gz")
    position = jnp.transpose(positions[0, 0], (1, 0, 2))
    velocity = jnp.transpose(velocities[0, 0], (1, 0, 2))
    mass = masses[0, 0]
    counts = tile_counts[0]
    listed = jnp.transpose(neighbour_list[0, 0], (1, 0))

    tile_shape = (4, TZ, 128)
    modes, packed, live = call(
        deposit_kernel,
        [(PY, 8, 128), tile_shape, (TZ, 128)],
        (counts, position, mass, t["fwd_z"]),
        spaces="hhhh",
        scratch=[
            pltpu.SMEM((1, TZ), jnp.int32),
            pltpu.VMEM((3, TZ, 128), f32),
            pltpu.VMEM((TZ, 128), f32),
            pltpu.VMEM((8, 256, 256), bf16),
            pltpu.SemaphoreType.DMA((4,)),
        ],
        room=63_400_000,
    )
    modes = exchange(modes, "gy").reshape(PY * 8, 128)
    packed = packed.reshape(4 * TZ, 128)
    (modes,) = call(forward_y_kernel, [(4 * PX, 128)], (modes, *t["fwd_y"], packed))
    modes = exchange(modes.reshape(PX, 4, 128), wide).reshape(4 * PX, 128)
    waves = (t["kappa_x"], t["kappa_y"], t["kappa_z"])
    (fields,) = call(
        solve_x_kernel, [(8 * PX, 128)], (modes, *t["fwd_x"], *t["inv_x"], *waves)
    )
    fields = exchange(fields.reshape(PX, 8, 128), wide).reshape(8 * PX, 128)
    fields, row = call(
        inverse_y_kernel,
        [(PY * 3 * CY, 128), (3, 4 * TZ, 128)],
        (fields, *t["inv_y"], packed),
    )
    row = row.reshape(3, 4, TZ, 128)
    left = shift(row, "gy", PY, 1)
    right = shift(row, "gy", PY, -1)
    fields = exchange(fields.reshape(PY, 3 * CY // 2, 2, 128), "gy").reshape(PY * 3 * CY, 128)
    short = short_range(listed, left, row, right)
    (kicked,) = call(
        kick_kernel,
        [(3, TZ, 128)],
        (live, fields, position, velocity, short, t["inv_z"], t["sine_z"]),
    )
    return jnp.transpose(kicked, (1, 0, 2))[None, None]


def solution(mesh):
    wide = ("gx", "gz")
    placed = (
        P(wide, "gy", None, None, None),
        P(wide, "gy", None, None),
        P(wide, "gy", None, None, None),
        P(wide, "gy", None),
        P(wide, "gy", None, None),
    )
    return jax.shard_map(
        shards,
        mesh=mesh,
        in_specs=placed,
        out_specs=P(wide, "gy", None, None, None),
        check_vma=False,
    )
```

```python
import functools

import jax
import jax.numpy as jnp
import ml_dtypes
import numpy as np
from jax import lax
from jax.experimental import pallas as pl
from jax.experimental.pallas import tpu as pltpu
from jax.sharding import PartitionSpec as P

CX = 2
CY = 6
NZ = 1024
TZ = 16
NB = 6
NX = 96
NY = 96
PX = 48
PY = 16
CELLS = NZ // TZ
BLOCK = NZ // PY
HALF = BLOCK // 2
PIECES = 4 * TZ // 2

smoothing = 0.1
screening = 0.01
split_scale = 2.0
softening = 0.05
long_kick = 1.0
short_kick = 0.05

f32 = jnp.float32
bf16 = jnp.bfloat16


def halves(table):
    high = table.astype(np.float32).astype(ml_dtypes.bfloat16)
    low = (table - high.astype(np.float64)).astype(np.float32).astype(ml_dtypes.bfloat16)
    return high, low


def real_basis(length, run):
    cells = np.arange(length)[:, None]
    wave = np.arange(length // 2)
    angle = 2 * np.pi * (cells * wave[None] % length) / length
    cosine = np.cos(angle) * np.sqrt(2 / length)
    sine = np.sin(angle) * np.sqrt(2 / length)
    step = np.sin(2 * np.pi * wave / length)
    cos_slope = sine * step
    sin_slope = -cosine * step
    cosine[:, 0] = np.sqrt(1 / length)
    sine[:, 0] = np.where(cells[:, 0] % 2 == 0, 1.0, -1.0) * np.sqrt(1 / length)
    cos_slope[:, 0] = 0
    sin_slope[:, 0] = 0
    kappa_cos = 4 * np.sin(np.pi * wave / length) ** 2
    kappa_sin = kappa_cos.copy()
    kappa_sin[0] = 4.0

    def laid(first, second):
        shape = first.shape[:-1] + (-1, 1, run)
        return np.concatenate([first.reshape(shape), second.reshape(shape)], axis=-2).reshape(
            first.shape[:-1] + (length,)
        )

    return (
        laid(cosine, sine),
        laid(cos_slope, sin_slope),
        laid(kappa_cos, kappa_sin),
        laid(-step, step),
    )


def depth_basis():
    table = np.zeros((4, 2, 128, 256))
    waves = np.zeros((4, 128))
    waves[0] = np.concatenate([8 * np.arange(64), 8 * np.arange(64) + 4])
    for residue in (1, 2, 3):
        waves[residue] = 8 * np.arange(128) + residue
    angle = 2 * np.pi * (np.arange(128)[:, None] * waves[:, None] % NZ) / NZ
    cosine = np.cos(angle) * np.sqrt(2 / NZ)
    sine = np.sin(angle) * np.sqrt(2 / NZ)
    cosine[0, :, 0] = np.sqrt(1 / NZ)
    sine[0, :, 0] = np.where(np.arange(128) % 2 == 0, 1.0, -1.0) * np.sqrt(1 / NZ)
    step = np.sin(2 * np.pi * waves / NZ)
    kappa_cos = 4 * np.sin(np.pi * waves / NZ) ** 2
    kappa_sin = kappa_cos.copy()
    step[0, 0] = 0
    kappa_sin[0, 0] = 4.0

    def laid(first, second):
        shape = first.shape[:-1] + (4, 1, HALF)
        return np.concatenate([first.reshape(shape), second.reshape(shape)], axis=-2).reshape(
            first.shape[:-1] + (256,)
        )

    table[:, 0] = laid(cosine, sine)
    table[:, 1] = laid(-sine, cosine)
    table[0, 1, :, 128:] = table[0, 0, :, 128:]
    table[0, 0, :, 128:] = 0
    table[0, 1, :, :128] = 0
    return (
        table.reshape(4, 256, 256),
        laid(kappa_cos, kappa_sin).reshape(NZ),
        laid(-step, step).reshape(NZ),
    )


ROOT_HALF = float(np.sqrt(0.5))


def waves_of(cells):
    total = [cells[a] + cells[a + 4] for a in range(4)]
    apart = [cells[a] - cells[a + 4] for a in range(4)]
    even, odd = total[0] + total[2], total[1] + total[3]
    less, more = (apart[1] - apart[3]) * ROOT_HALF, (apart[1] + apart[3]) * ROOT_HALF
    pairs = (
        (even + odd, even - odd),
        (apart[0] + less, more + apart[2]),
        (total[0] - total[2], total[1] - total[3]),
        (apart[0] - less, more - apart[2]),
    )
    return [jnp.concatenate(pair, axis=1) for pair in pairs]


def cells_of(pairs):
    (zero, four), one, two, three = [(pair[:, :128], pair[:, 128:]) for pair in pairs]
    plus, minus = zero + four, zero - four
    even = (plus + two[0], minus + two[1], plus - two[0], minus - two[1])
    less, more = (one[0] - three[0]) * ROOT_HALF, (one[1] + three[1]) * ROOT_HALF
    odd = (one[0] + three[0], more + less, one[1] - three[1], more - less)
    return [even[a] + odd[a] for a in range(4)] + [even[a] - odd[a] for a in range(4)]


@functools.lru_cache(None)
def tables():
    table_z, kappa_z, sine_z = depth_basis()
    basis_x, slope_x, kappa_x, _ = real_basis(NX, 1)
    basis_y, slope_y, kappa_y, _ = real_basis(NY, 1)
    out = {}
    out["fwd_z"] = np.concatenate(halves(table_z), axis=0)
    out["inv_z"] = np.concatenate(halves(table_z.transpose(0, 2, 1)), axis=0)
    pad_y = np.zeros((2, PX, PY, 8))
    pad_y[..., :CY] = basis_y.T.reshape(PX, 2, PY, CY).transpose(1, 0, 2, 3)
    out["fwd_y"] = halves(pad_y.reshape(NY, PY * 8))
    out["fwd_x"] = halves(basis_x.reshape(PX, CX, NX).transpose(2, 1, 0).reshape(NX, CX * PX))
    both = np.stack([slope_x.reshape(PX, CX, NX), basis_x.reshape(PX, CX, NX)])
    out["inv_x"] = halves(both.transpose(0, 2, 1, 3).reshape(2 * CX * PX, NX))

    rows = np.zeros((2, PY, 3, CY, 2, PX))
    spread = [table.reshape(PY, CY, PX, 2).transpose(3, 0, 1, 2) for table in (basis_y, slope_y)]
    rows[:, :, 0, :, 0] = spread[0]
    rows[:, :, 1, :, 1] = spread[1]
    rows[:, :, 2, :, 1] = spread[0]
    out["inv_y"] = halves(rows.reshape(2 * PY * 3 * CY, 2 * PX))
    out["kappa_x"] = kappa_x[:, None].astype(np.float32)
    out["kappa_y"] = np.repeat(kappa_y.reshape(PX, 2), BLOCK, axis=1).astype(np.float32)
    out["kappa_z"] = np.tile(kappa_z.reshape(PY, BLOCK), (1, 2)).astype(np.float32)
    out["sine_z"] = np.tile(sine_z.reshape(PY, BLOCK), (1, 2)).astype(np.float32)
    return out


def split(value):
    high = value.astype(bf16)
    return high, (value - high.astype(f32)).astype(bf16)


def dot(left, right):
    return lax.dot_general(left, right, (((1,), (0,)), ((), ())), preferred_element_type=f32)


def dot_t(left, right):
    return lax.dot_general(left, right, (((1,), (1,)), ((), ())), preferred_element_type=f32)


def table_dot(high_ref, low_ref, value):
    lanes = value.shape[1]
    high, low = split(value)
    both = dot(high_ref[...], jnp.concatenate([high, low], axis=1))
    return both[:, :lanes] + both[:, lanes:] + dot(low_ref[...], high)


def dot_table(value, table_ref, at):
    rows = value.shape[0]
    high, low = split(value)
    both = dot(jnp.concatenate([high, low], axis=0), table_ref[at])
    return both[:rows] + both[rows:] + dot(high, table_ref[4 + at])


def iota(shape, dim):
    return lax.broadcasted_iota(jnp.int32, shape, dim)


def plane_weights(pos_ref, tile):
    row = iota((16, 128), 0)
    row_x = (row >> 3).astype(f32)
    row_y = (row & 7).astype(f32)
    x = jnp.clip(pos_ref[0, tile : tile + 1, :] * CX - 0.5, 0.0, 1.0)
    y = jnp.clip(pos_ref[1, tile : tile + 1, :] * CY - 0.5, 0.0, CY - 1.0)
    return (1.0 - jnp.abs(x - row_x)) * jnp.maximum(1.0 - jnp.abs(y - row_y), 0.0)


def depth_weights(pos_ref, tile):
    z = (tile + pos_ref[2, tile : tile + 1, :]) * CELLS - 0.5 - (tile * CELLS - CELLS // 2)
    return jnp.maximum(1.0 - jnp.abs(z - iota((128, 128), 0).astype(f32)), 0.0)


def deposit_kernel(
    counts_hbm,
    pos_hbm,
    mass_hbm,
    table_hbm,
    sine_hbm,
    out_ref,
    packed_ref,
    live_ref,
    counts,
    pos_ref,
    mass_ref,
    table_ref,
    arrived,
):
    loads = [
        pltpu.make_async_copy(source, held, arrived.at[at])
        for at, (source, held) in enumerate(
            (
                (counts_hbm, counts),
                (pos_hbm, pos_ref),
                (mass_hbm, mass_ref),
                (table_hbm, table_ref),
                (sine_hbm, live_ref.at[TZ : TZ + PY]),
            )
        )
    ]
    for load in loads:
        load.start()
    for load in loads[:3]:
        load.wait()
    packed_ref[:3] = pos_ref[...]
    slot = iota((1, 128), 1)
    windows = []
    for tile in range(TZ):
        live = slot < counts[0, tile]
        live_ref[tile : tile + 1, :] = jnp.where(live, 1.0, 0.0)
        mass = jnp.where(live, mass_ref[tile : tile + 1, :], 0.0)
        packed_ref[3, tile : tile + 1, :] = mass
        flat_high, flat_low = split(plane_weights(pos_ref, tile) * mass)
        deep_high, deep_low = split(depth_weights(pos_ref, tile))
        both = dot_t(jnp.concatenate([flat_high, flat_low], axis=0), deep_high)
        windows.append(both[:16] + both[16:] + dot_t(flat_high, deep_low))
    even = jnp.concatenate(windows[0::2], axis=1)
    odd = jnp.concatenate(windows[1::2], axis=1)
    density = pltpu.roll(even, NZ - CELLS // 2, 1) + pltpu.roll(odd, CELLS // 2, 1)
    pairs = waves_of([density[:, 128 * a : 128 * a + 128] for a in range(8)])
    for load in loads[3:]:
        load.wait()
    modes = [dot_table(value, table_ref, at) for at, value in enumerate(pairs)]
    first = iota((8, 128), 1) < BLOCK
    for pair in range(PY // 2):
        part = modes[pair // 2][:, 128 * (pair % 2) : 128 * (pair % 2) + 128]
        near = part[:8]
        far = part[8:]
        out_ref[2 * pair] = jnp.where(first, near, pltpu.roll(far, BLOCK, 1))
        out_ref[2 * pair + 1] = jnp.where(first, pltpu.roll(near, BLOCK, 1), far)


def forward_y_kernel(in_ref, high_ref, low_ref, packed_ref, out_ref):
    value = table_dot(high_ref, low_ref, in_ref[...])
    for at in range(2):
        out_ref[pl.ds(at, PX, stride=4), :] = value[PX * at : PX * (at + 1)]
        out_ref[pl.ds(2 + at, PIECES, stride=4), :] = packed_ref[pl.ds(at, PIECES, stride=2), :]
        out_ref[pl.ds(4 * PIECES + 2 + at, PX - PIECES, stride=4), :] = jnp.zeros(
            (PX - PIECES, 128), f32
        )


def solve_x_kernel(
    in_ref, fwd_high, fwd_low, inv_high, inv_low, kappa_x, kappa_y, kappa_z, out_ref
):
    at_x = lax.axis_index(("gx", "gz"))
    at_y = lax.axis_index("gy")
    first = iota((PX, 128), 1) < BLOCK
    wave_a = in_ref[pl.ds(0, PX, stride=4), :]
    wave_b = in_ref[pl.ds(1, PX, stride=4), :]
    cells_0 = jnp.where(first, wave_a, pltpu.roll(wave_b, BLOCK, 1))
    cells_1 = jnp.where(first, pltpu.roll(wave_a, BLOCK, 1), wave_b)
    spectrum = table_dot(fwd_high, fwd_low, jnp.concatenate([cells_0, cells_1], axis=0))
    kappa_sum = kappa_x[...] + (kappa_y[pl.ds(at_x, 1), :] + kappa_z[pl.ds(at_y, 1), :])
    potential = spectrum * (-jnp.exp(-smoothing * kappa_sum) / (kappa_sum + screening))
    fields = table_dot(inv_high, inv_low, potential)
    for at in range(4):
        out_ref[pl.ds(at, PX, stride=8), :] = fields[PX * at : PX * (at + 1)]
    for at in range(2):
        piece = in_ref[pl.ds(2 + at, PX, stride=4), :]
        out_ref[pl.ds(4 + at, PX, stride=8), :] = pltpu.roll(piece, 1, 0)
        out_ref[pl.ds(6 + at, PX, stride=8), :] = pltpu.roll(piece, PX - 1, 0)


def inverse_y_kernel(in_ref, high_ref, low_ref, packed_ref, out_ref, row_ref):
    rows = PY * 3 * CY
    first = iota((rows, 128), 1) < BLOCK
    cells = [
        jnp.concatenate([in_ref[pl.ds(at, PX, stride=8), :] for at in (x, x + 2)], axis=0)
        for x in range(CX)
    ]
    value = table_dot(high_ref, low_ref, jnp.concatenate(cells, axis=1))
    cos_0, cos_1 = value[:rows, :128], value[:rows, 128:]
    sin_0, sin_1 = value[rows:, :128], value[rows:, 128:]
    cell_0 = cos_0 + pltpu.roll(sin_0, BLOCK, 1)
    cell_1 = pltpu.roll(cos_1, BLOCK, 1) + sin_1
    out_ref[...] = jnp.where(first, cell_0, cell_1)
    row_ref[1] = packed_ref[...]
    for at in range(2):
        for side in range(2):
            row_ref[2 * side, pl.ds(at, PIECES, stride=2), :] = in_ref[
                pl.ds(4 + 2 * side + at, PIECES, stride=8), :
            ]


def kick_kernel(
    live_ref, in_ref, vel_ref, short_ref, deep_ref, flat_ref, table_ref, out_ref
):
    first = iota((24, 128), 1) < BLOCK
    cosines = (iota((8, 128), 1) & (BLOCK - 1)) < HALF

    def block(at):
        last = PY * 3 * CY - 8
        parts = []
        for row in range(3 * CY * at, 3 * CY * (at + 1), CY):
            part = in_ref[min(row, last) : min(row, last) + 8, :]
            parts.append(part if row <= last else pltpu.roll(part, 8 - (row - last), 0))
        turned = jnp.where(
            cosines, pltpu.roll(parts[2], 128 - HALF, 1), pltpu.roll(parts[2], HALF, 1)
        )
        return jnp.concatenate(parts[:2] + [turned * live_ref[TZ + at : TZ + at + 1, :]], axis=0)

    near, far = [], []
    for pair in range(PY // 2):
        a, b = block(2 * pair), block(2 * pair + 1)
        near.append(jnp.where(first, a, pltpu.roll(b, BLOCK, 1)))
        far.append(jnp.where(first, pltpu.roll(a, BLOCK, 1), b))
    modes = [jnp.concatenate(parts, axis=0) for parts in zip(near, far)]
    pairs = [
        dot_table(jnp.concatenate(modes[2 * at : 2 * at + 2], axis=1), table_ref, at)
        for at in range(4)
    ]
    forces = jnp.concatenate(cells_of(pairs), axis=1)
    shifted = (
        pltpu.roll(forces, CELLS // 2, 1),
        pltpu.roll(forces, NZ - CELLS // 2, 1),
    )
    for tile in range(TZ):
        start = 128 * (tile // 2)
        window = shifted[tile % 2][:, start : start + 128]
        high, low = split(window)
        both = dot(jnp.concatenate([high, low], axis=0), deep_ref[0, tile])
        picked = both[:48] + both[48:] + dot(high, deep_ref[1, tile])
        flat = flat_ref[tile]
        live = live_ref[tile : tile + 1, :]
        for comp in range(3):
            at = 8 * comp
            total = flat[:8] * picked[at : at + 8] + flat[8:] * picked[24 + at : 32 + at]
            long_accel = jnp.sum(total, axis=0, keepdims=True)
            kick = long_kick * long_accel + short_kick * short_ref[comp, tile : tile + 1, :]
            out_ref[comp, tile : tile + 1, :] = vel_ref[comp, tile : tile + 1, :] + live * kick


def short_kernel(
    listed, left_ref, mid_ref, right_ref, out_ref, deep_ref, flat_ref, shell, sums_even, sums_odd
):
    pos_ref = mid_ref.at[1]
    for tile in range(TZ):
        flat_ref[tile] = plane_weights(pos_ref, tile)
        deep_ref[0, tile], deep_ref[1, tile] = split(depth_weights(pos_ref, tile))
    for at, ref in enumerate((left_ref, mid_ref, right_ref)):
        for dx in range(3):
            shell[3 * dx + at] = ref[dx]

    def pairs(tile, sums):
        rows = [shell[4, comp, pl.ds(tile, 1), :] for comp in range(3)]
        columns = jnp.concatenate(rows + [jnp.zeros((5, 128), f32)], axis=0).T
        sources = []
        for entry in range(NB):
            code = listed[entry, tile]
            group = code >> 4
            layer = code & (TZ - 1)
            step_x = (group * 11) >> 5
            step_y = group - 3 * step_x
            step_z = (layer - tile + 1) & (TZ - 1)
            shifts = [(step - 1).astype(f32) for step in (step_x, step_y, step_z)]
            source = [shell[group, comp, pl.ds(layer, 1), :] for comp in range(4)]
            sources.append([source[comp] + shifts[comp] for comp in range(3)] + [source[3]])
        for chunk in range(16):
            part = slice(8 * chunk, 8 * chunk + 8)
            own = [jnp.broadcast_to(columns[part, comp : comp + 1], (8, 128)) for comp in range(3)]
            totals = [None] * 3
            for x, y, z, mass in sources:
                apart = [x - own[0], y - own[1], z - own[2]]
                square = apart[0] * apart[0] + apart[1] * apart[1] + apart[2] * apart[2]
                root = lax.rsqrt(square + softening)
                strength = (mass * jnp.exp(square * (-1.0 / split_scale))) * (root * root * root)
                for comp in range(3):
                    term = strength * apart[comp]
                    totals[comp] = term if totals[comp] is None else totals[comp] + term
            for comp in range(3):
                sums[128 * comp + 8 * chunk : 128 * comp + 8 * chunk + 8, :] = totals[comp]

    def add_up(tile, sums):
        ones = jnp.ones((8, 128), bf16)
        high, low = split(sums[...])
        total = dot_t(ones, high) + dot_t(ones, low)
        for comp in range(3):
            out_ref[comp, pl.ds(tile, 1), :] = total[:1, 128 * comp : 128 * comp + 128]

    def two(at, carry):
        add_up(2 * at, sums_even)
        pairs(2 * at + 1, sums_odd)
        add_up(2 * at + 1, sums_odd)
        pairs(2 * at + 2, sums_even)
        return carry

    pairs(0, sums_even)
    lax.fori_loop(0, TZ // 2 - 1, two, 0)
    add_up(TZ - 2, sums_even)
    pairs(TZ - 1, sums_odd)
    add_up(TZ - 1, sums_odd)


def call(kernel, shapes, operands, spaces="", scratch=(), cost=None, room=24 << 20):
    space_of = {"s": pltpu.SMEM, "h": pltpu.HBM, "a": pl.ANY, "v": pltpu.VMEM}
    spaces = spaces.ljust(len(operands), "v")
    shapes = [shape if isinstance(shape[0], tuple) else (shape, f32) for shape in shapes]
    return pl.pallas_call(
        kernel,
        out_shape=[jax.ShapeDtypeStruct(*shape) for shape in shapes],
        in_specs=[pl.BlockSpec(memory_space=space_of[space]) for space in spaces],
        out_specs=[pl.BlockSpec(memory_space=pltpu.VMEM)] * len(shapes),
        scratch_shapes=scratch,
        cost_estimate=cost,
        compiler_params=pltpu.CompilerParams(vmem_limit_bytes=room),
    )(*operands)


def exchange(value, axis):
    return lax.all_to_all(value, axis, split_axis=0, concat_axis=0, tiled=True)


def shift(value, axis, count, step):
    return lax.ppermute(value, axis, [(i, (i + step) % count) for i in range(count)])


def short_range(*operands):
    pairs = TZ * NB * 128 * 128
    return call(
        short_kernel,
        [(3, TZ, 128), ((2, TZ, 128, 128), bf16), (TZ, 16, 128)],
        operands,
        spaces="s",
        scratch=[pltpu.VMEM((9, 4, TZ, 128), f32)] + [pltpu.VMEM((3 * 128, 128), f32)] * 2,
        cost=pl.CostEstimate(flops=40_000 * pairs, bytes_accessed=400_000, transcendentals=2 * pairs),
    )


def shards(positions, masses, velocities, tile_counts, neighbour_list):
    t = tables()
    wide = ("gx", "gz")
    position = jnp.transpose(positions[0, 0], (1, 0, 2))
    velocity = jnp.transpose(velocities[0, 0], (1, 0, 2))
    mass = masses[0, 0]
    counts = tile_counts[0]
    listed = jnp.transpose(neighbour_list[0, 0], (1, 0))

    tile_shape = (4, TZ, 128)
    modes, packed, live = call(
        deposit_kernel,
        [(PY, 8, 128), tile_shape, (TZ + PY, 128)],
        (counts, position, mass, t["fwd_z"], t["sine_z"]),
        spaces="hhhhh",
        scratch=[
            pltpu.SMEM((1, TZ), jnp.int32),
            pltpu.VMEM((3, TZ, 128), f32),
            pltpu.VMEM((TZ, 128), f32),
            pltpu.VMEM((8, 256, 256), bf16),
            pltpu.SemaphoreType.DMA((5,)),
        ],
        room=63_400_000,
    )
    modes = exchange(modes, "gy").reshape(PY * 8, 128)
    packed = packed.reshape(4 * TZ, 128)
    (modes,) = call(forward_y_kernel, [(4 * PX, 128)], (modes, *t["fwd_y"], packed))
    modes = exchange(modes.reshape(PX, 4, 128), wide).reshape(4 * PX, 128)
    waves = (t["kappa_x"], t["kappa_y"], t["kappa_z"])
    (fields,) = call(
        solve_x_kernel, [(8 * PX, 128)], (modes, *t["fwd_x"], *t["inv_x"], *waves)
    )
    fields = exchange(fields.reshape(PX, 8, 128), wide).reshape(8 * PX, 128)
    fields, row = call(
        inverse_y_kernel,
        [(PY * 3 * CY, 128), (3, 4 * TZ, 128)],
        (fields, *t["inv_y"], packed),
    )
    row = row.reshape(3, 4, TZ, 128)
    left = shift(row, "gy", PY, 1)
    right = shift(row, "gy", PY, -1)
    fields = exchange(fields.reshape(PY, 3 * CY // 2, 2, 128), "gy").reshape(PY * 3 * CY, 128)
    short, deep, flat = short_range(listed, left, row, right)
    (kicked,) = call(
        kick_kernel,
        [(3, TZ, 128)],
        (live, fields, velocity, short, deep, flat, t["inv_z"]),
    )
    return jnp.transpose(kicked, (1, 0, 2))[None, None]


def solution(mesh):
    wide = ("gx", "gz")
    placed = (
        P(wide, "gy", None, None, None),
        P(wide, "gy", None, None),
        P(wide, "gy", None, None, None),
        P(wide, "gy", None),
        P(wide, "gy", None, None),
    )
    return jax.shard_map(
        shards,
        mesh=mesh,
        in_specs=placed,
        out_specs=P(wide, "gy", None, None, None),
        check_vma=False,
    )
```

```python
import functools

import jax
import jax.numpy as jnp
import ml_dtypes
import numpy as np
from jax import lax
from jax.experimental import pallas as pl
from jax.experimental.pallas import tpu as pltpu
from jax.sharding import PartitionSpec as P

CX = 2
CY = 6
NZ = 1024
TZ = 16
NB = 6
NX = 96
NY = 96
PX = 48
PY = 16
CELLS = NZ // TZ
BLOCK = NZ // PY
HALF = BLOCK // 2
REST = 4 * TZ - PX

smoothing = 0.1
screening = 0.01
split_scale = 2.0
softening = 0.05
long_kick = 1.0
short_kick = 0.05

f32 = jnp.float32
bf16 = jnp.bfloat16


def halves(table):
    high = table.astype(np.float32).astype(ml_dtypes.bfloat16)
    low = (table - high.astype(np.float64)).astype(np.float32).astype(ml_dtypes.bfloat16)
    return high, low


def real_basis(length, run):
    cells = np.arange(length)[:, None]
    wave = np.arange(length // 2)
    angle = 2 * np.pi * (cells * wave[None] % length) / length
    cosine = np.cos(angle) * np.sqrt(2 / length)
    sine = np.sin(angle) * np.sqrt(2 / length)
    step = np.sin(2 * np.pi * wave / length)
    cos_slope = sine * step
    sin_slope = -cosine * step
    cosine[:, 0] = np.sqrt(1 / length)
    sine[:, 0] = np.where(cells[:, 0] % 2 == 0, 1.0, -1.0) * np.sqrt(1 / length)
    cos_slope[:, 0] = 0
    sin_slope[:, 0] = 0
    kappa_cos = 4 * np.sin(np.pi * wave / length) ** 2
    kappa_sin = kappa_cos.copy()
    kappa_sin[0] = 4.0

    def laid(first, second):
        shape = first.shape[:-1] + (-1, 1, run)
        return np.concatenate([first.reshape(shape), second.reshape(shape)], axis=-2).reshape(
            first.shape[:-1] + (length,)
        )

    return (
        laid(cosine, sine),
        laid(cos_slope, sin_slope),
        laid(kappa_cos, kappa_sin),
        laid(-step, step),
    )


def depth_basis():
    table = np.zeros((4, 2, 128, 256))
    waves = np.zeros((4, 128))
    waves[0] = np.concatenate([8 * np.arange(64), 8 * np.arange(64) + 4])
    for residue in (1, 2, 3):
        waves[residue] = 8 * np.arange(128) + residue
    angle = 2 * np.pi * (np.arange(128)[:, None] * waves[:, None] % NZ) / NZ
    cosine = np.cos(angle) * np.sqrt(2 / NZ)
    sine = np.sin(angle) * np.sqrt(2 / NZ)
    cosine[0, :, 0] = np.sqrt(1 / NZ)
    sine[0, :, 0] = np.where(np.arange(128) % 2 == 0, 1.0, -1.0) * np.sqrt(1 / NZ)
    step = np.sin(2 * np.pi * waves / NZ)
    kappa_cos = 4 * np.sin(np.pi * waves / NZ) ** 2
    kappa_sin = kappa_cos.copy()
    step[0, 0] = 0
    kappa_sin[0, 0] = 4.0

    def laid(first, second):
        shape = first.shape[:-1] + (4, 1, HALF)
        return np.concatenate([first.reshape(shape), second.reshape(shape)], axis=-2).reshape(
            first.shape[:-1] + (256,)
        )

    table[:, 0] = laid(cosine, sine)
    table[:, 1] = laid(-sine, cosine)
    table[0, 1, :, 128:] = table[0, 0, :, 128:]
    table[0, 0, :, 128:] = 0
    table[0, 1, :, :128] = 0
    return (
        table.reshape(4, 256, 256),
        laid(kappa_cos, kappa_sin).reshape(NZ),
        laid(-step, step).reshape(NZ),
    )


ROOT_HALF = float(np.sqrt(0.5))


def waves_of(cells):
    total = [cells[a] + cells[a + 4] for a in range(4)]
    apart = [cells[a] - cells[a + 4] for a in range(4)]
    even, odd = total[0] + total[2], total[1] + total[3]
    less, more = (apart[1] - apart[3]) * ROOT_HALF, (apart[1] + apart[3]) * ROOT_HALF
    pairs = (
        (even + odd, even - odd),
        (apart[0] + less, more + apart[2]),
        (total[0] - total[2], total[1] - total[3]),
        (apart[0] - less, more - apart[2]),
    )
    return [jnp.concatenate(pair, axis=1) for pair in pairs]


def cells_of(pairs):
    (zero, four), one, two, three = [(pair[:, :128], pair[:, 128:]) for pair in pairs]
    plus, minus = zero + four, zero - four
    even = (plus + two[0], minus + two[1], plus - two[0], minus - two[1])
    less, more = (one[0] - three[0]) * ROOT_HALF, (one[1] + three[1]) * ROOT_HALF
    odd = (one[0] + three[0], more + less, one[1] - three[1], more - less)
    return [even[a] + odd[a] for a in range(4)] + [even[a] - odd[a] for a in range(4)]


@functools.lru_cache(None)
def tables():
    table_z, kappa_z, sine_z = depth_basis()
    basis_x, slope_x, kappa_x, _ = real_basis(NX, 1)
    basis_y, slope_y, kappa_y, _ = real_basis(NY, 1)
    out = {}
    out["fwd_z"] = np.concatenate(halves(table_z), axis=0)
    out["inv_z"] = np.concatenate(halves(table_z.transpose(0, 2, 1)), axis=0)
    out["fwd_y"] = halves(basis_y.T.reshape(PX, 2, NY).transpose(1, 0, 2).reshape(NY, NY))
    out["fwd_x"] = halves(basis_x.reshape(PX, CX, NX).transpose(2, 1, 0).reshape(NX, CX * PX))
    both = np.stack([slope_x.reshape(PX, CX, NX), basis_x.reshape(PX, CX, NX)])
    out["inv_x"] = halves(both.transpose(0, 2, 1, 3).reshape(2 * CX * PX, NX))

    rows = np.zeros((2, PY, 3, CY, 2, PX))
    spread = [table.reshape(PY, CY, PX, 2).transpose(3, 0, 1, 2) for table in (basis_y, slope_y)]
    rows[:, :, 0, :, 0] = spread[0]
    rows[:, :, 1, :, 1] = spread[1]
    rows[:, :, 2, :, 1] = spread[0]
    out["inv_y"] = halves(rows.reshape(2 * PY * 3 * CY, 2 * PX))
    out["kappa_x"] = kappa_x[:, None].astype(np.float32)
    out["kappa_y"] = np.repeat(kappa_y.reshape(PX, 2), BLOCK, axis=1).astype(np.float32)
    out["kappa_z"] = np.tile(kappa_z.reshape(PY, BLOCK), (1, 2)).astype(np.float32)
    out["sine_z"] = np.tile(sine_z.reshape(PY, BLOCK), (1, 2)).astype(np.float32)
    return out


def split(value):
    high = value.astype(bf16)
    return high, (value - high.astype(f32)).astype(bf16)


def dot(left, right):
    return lax.dot_general(left, right, (((1,), (0,)), ((), ())), preferred_element_type=f32)


def dot_t(left, right):
    return lax.dot_general(left, right, (((1,), (1,)), ((), ())), preferred_element_type=f32)


def table_dot(high_ref, low_ref, value):
    lanes = value.shape[1]
    high, low = split(value)
    both = dot(high_ref[...], jnp.concatenate([high, low], axis=1))
    return both[:, :lanes] + both[:, lanes:] + dot(low_ref[...], high)


def dot_table(value, table_ref, at):
    rows = value.shape[0]
    high, low = split(value)
    both = dot(jnp.concatenate([high, low], axis=0), table_ref[at])
    return both[:rows] + both[rows:] + dot(high, table_ref[4 + at])


def iota(shape, dim):
    return lax.broadcasted_iota(jnp.int32, shape, dim)


def plane_weights(pos_ref, tile):
    row = iota((16, 128), 0)
    row_x = (row >> 3).astype(f32)
    row_y = (row & 7).astype(f32)
    x = jnp.clip(pos_ref[0, tile : tile + 1, :] * CX - 0.5, 0.0, 1.0)
    y = jnp.clip(pos_ref[1, tile : tile + 1, :] * CY - 0.5, 0.0, CY - 1.0)
    return (1.0 - jnp.abs(x - row_x)) * jnp.maximum(1.0 - jnp.abs(y - row_y), 0.0)


def depth_weights(pos_ref, tile):
    z = (tile + pos_ref[2, tile : tile + 1, :]) * CELLS - 0.5 - (tile * CELLS - CELLS // 2)
    return jnp.maximum(1.0 - jnp.abs(z - iota((128, 128), 0).astype(f32)), 0.0)


def deposit_kernel(
    counts_hbm,
    pos_hbm,
    mass_hbm,
    table_hbm,
    sine_hbm,
    out_ref,
    packed_ref,
    live_ref,
    counts,
    pos_ref,
    mass_ref,
    table_ref,
    arrived,
):
    loads = [
        pltpu.make_async_copy(source, held, arrived.at[at])
        for at, (source, held) in enumerate(
            (
                (counts_hbm, counts),
                (pos_hbm, pos_ref),
                (mass_hbm, mass_ref),
                (table_hbm, table_ref),
                (sine_hbm, live_ref.at[TZ : TZ + PY]),
            )
        )
    ]
    for load in loads:
        load.start()
    for load in loads[:3]:
        load.wait()
    packed_ref[:3] = pos_ref[...]
    slot = iota((1, 128), 1)
    windows = []
    for tile in range(TZ):
        live = slot < counts[0, tile]
        live_ref[tile : tile + 1, :] = jnp.where(live, 1.0, 0.0)
        mass = jnp.where(live, mass_ref[tile : tile + 1, :], 0.0)
        packed_ref[3, tile : tile + 1, :] = mass
        flat_high, flat_low = split(plane_weights(pos_ref, tile) * mass)
        deep_high, deep_low = split(depth_weights(pos_ref, tile))
        both = dot_t(jnp.concatenate([flat_high, flat_low], axis=0), deep_high)
        windows.append(both[:16] + both[16:] + dot_t(flat_high, deep_low))
    even = jnp.concatenate(windows[0::2], axis=1)
    odd = jnp.concatenate(windows[1::2], axis=1)
    density = pltpu.roll(even, NZ - CELLS // 2, 1) + pltpu.roll(odd, CELLS // 2, 1)
    pairs = waves_of([density[:, 128 * a : 128 * a + 128] for a in range(8)])
    for load in loads[3:]:
        load.wait()
    modes = [dot_table(value, table_ref, at) for at, value in enumerate(pairs)]
    first = iota((8, 128), 1) < BLOCK
    for pair in range(PY // 2):
        part = modes[pair // 2][:, 128 * (pair % 2) : 128 * (pair % 2) + 128]
        near = part[:8]
        far = part[8:]
        blocks = (
            jnp.where(first, near, pltpu.roll(far, BLOCK, 1)),
            jnp.where(first, pltpu.roll(near, BLOCK, 1), far),
        )
        for at, block in enumerate(blocks):
            start = CY * (2 * pair + at)
            out_ref[start : start + CY, :] = block[:CY]


def forward_y_kernel(in_ref, high_ref, low_ref, packed_ref, out_ref):
    value = table_dot(high_ref, low_ref, in_ref[...])
    for at in range(2):
        out_ref[pl.ds(at, PX, stride=4), :] = value[PX * at : PX * (at + 1)]
        out_ref[pl.ds(3 + 4 * at, REST, stride=8), :] = packed_ref[PX:, :]
    out_ref[pl.ds(2, PX, stride=4), :] = packed_ref[:PX, :]
    out_ref[pl.ds(8 * REST + 3, PX - 2 * REST, stride=4), :] = jnp.zeros((PX - 2 * REST, 128), f32)


def solve_x_kernel(
    in_ref, fwd_high, fwd_low, inv_high, inv_low, kappa_x, kappa_y, kappa_z, out_ref
):
    at_x = lax.axis_index(("gx", "gz"))
    at_y = lax.axis_index("gy")
    first = iota((PX, 128), 1) < BLOCK
    wave_a = in_ref[pl.ds(0, PX, stride=4), :]
    wave_b = in_ref[pl.ds(1, PX, stride=4), :]
    cells_0 = jnp.where(first, wave_a, pltpu.roll(wave_b, BLOCK, 1))
    cells_1 = jnp.where(first, pltpu.roll(wave_a, BLOCK, 1), wave_b)
    spectrum = table_dot(fwd_high, fwd_low, jnp.concatenate([cells_0, cells_1], axis=0))
    kappa_sum = kappa_x[...] + (kappa_y[pl.ds(at_x, 1), :] + kappa_z[pl.ds(at_y, 1), :])
    potential = spectrum * (-jnp.exp(-smoothing * kappa_sum) / (kappa_sum + screening))
    fields = table_dot(inv_high, inv_low, potential)
    for at in range(4):
        out_ref[pl.ds(at, PX, stride=7), :] = fields[PX * at : PX * (at + 1)]
    piece = in_ref[pl.ds(2, PX, stride=4), :]
    out_ref[pl.ds(4, PX, stride=7), :] = pltpu.roll(piece, 1, 0)
    out_ref[pl.ds(5, PX, stride=7), :] = pltpu.roll(piece, PX - 1, 0)
    near = in_ref[pl.ds(3, PX, stride=4), :]
    far = pltpu.roll(near, BLOCK, 1)
    even = at_x % 2 == 0
    out_ref[pl.ds(6, PX, stride=7), :] = jnp.where(
        first,
        pltpu.roll(jnp.where(even, near, far), 1, 0),
        pltpu.roll(jnp.where(even, far, near), PX - 1, 0),
    )


def inverse_y_kernel(in_ref, high_ref, low_ref, packed_ref, out_ref, row_ref):
    rows = PY * 3 * CY
    first = iota((rows, 128), 1) < BLOCK
    cells = [
        jnp.concatenate([in_ref[pl.ds(at, PX, stride=7), :] for at in (x, x + 2)], axis=0)
        for x in range(CX)
    ]
    value = table_dot(high_ref, low_ref, jnp.concatenate(cells, axis=1))
    cos_0, cos_1 = value[:rows, :128], value[:rows, 128:]
    sin_0, sin_1 = value[rows:, :128], value[rows:, 128:]
    cell_0 = cos_0 + pltpu.roll(sin_0, BLOCK, 1)
    cell_1 = pltpu.roll(cos_1, BLOCK, 1) + sin_1
    out_ref[...] = jnp.where(first, cell_0, cell_1)
    row_ref[1] = packed_ref[...]
    row_ref[0, :PX, :] = in_ref[pl.ds(4, PX, stride=7), :]
    row_ref[2, :PX, :] = in_ref[pl.ds(5, PX, stride=7), :]
    low_half = first[:REST]
    one, two = in_ref[pl.ds(6, REST, stride=14), :], in_ref[pl.ds(13, REST, stride=14), :]
    row_ref[0, PX:, :] = jnp.where(low_half, one, pltpu.roll(two, BLOCK, 1))
    row_ref[2, PX:, :] = jnp.where(low_half, pltpu.roll(one, BLOCK, 1), two)


def kick_kernel(
    live_ref, in_ref, vel_ref, short_ref, deep_ref, flat_ref, table_ref, out_ref
):
    first = iota((24, 128), 1) < BLOCK
    cosines = (iota((8, 128), 1) & (BLOCK - 1)) < HALF

    def block(at):
        last = PY * 3 * CY - 8
        parts = []
        for row in range(3 * CY * at, 3 * CY * (at + 1), CY):
            part = in_ref[min(row, last) : min(row, last) + 8, :]
            parts.append(part if row <= last else pltpu.roll(part, 8 - (row - last), 0))
        turned = jnp.where(
            cosines, pltpu.roll(parts[2], 128 - HALF, 1), pltpu.roll(parts[2], HALF, 1)
        )
        return jnp.concatenate(parts[:2] + [turned * live_ref[TZ + at : TZ + at + 1, :]], axis=0)

    near, far = [], []
    for pair in range(PY // 2):
        a, b = block(2 * pair), block(2 * pair + 1)
        near.append(jnp.where(first, a, pltpu.roll(b, BLOCK, 1)))
        far.append(jnp.where(first, pltpu.roll(a, BLOCK, 1), b))
    modes = [jnp.concatenate(parts, axis=0) for parts in zip(near, far)]
    pairs = [
        dot_table(jnp.concatenate(modes[2 * at : 2 * at + 2], axis=1), table_ref, at)
        for at in range(4)
    ]
    forces = jnp.concatenate(cells_of(pairs), axis=1)
    shifted = (
        pltpu.roll(forces, CELLS // 2, 1),
        pltpu.roll(forces, NZ - CELLS // 2, 1),
    )
    for tile in range(TZ):
        start = 128 * (tile // 2)
        window = shifted[tile % 2][:, start : start + 128]
        high, low = split(window)
        both = dot(jnp.concatenate([high, low], axis=0), deep_ref[0, tile])
        picked = both[:48] + both[48:] + dot(high, deep_ref[1, tile])
        flat = flat_ref[tile]
        live = live_ref[tile : tile + 1, :]
        for comp in range(3):
            at = 8 * comp
            total = flat[:8] * picked[at : at + 8] + flat[8:] * picked[24 + at : 32 + at]
            long_accel = jnp.sum(total, axis=0, keepdims=True)
            kick = long_kick * long_accel + short_kick * short_ref[comp, tile : tile + 1, :]
            out_ref[comp, tile : tile + 1, :] = vel_ref[comp, tile : tile + 1, :] + live * kick


def short_kernel(
    listed, left_ref, mid_ref, right_ref, out_ref, deep_ref, flat_ref, shell, sums_even, sums_odd
):
    pos_ref = mid_ref.at[1]
    for tile in range(TZ):
        flat_ref[tile] = plane_weights(pos_ref, tile)
        deep_ref[0, tile], deep_ref[1, tile] = split(depth_weights(pos_ref, tile))
    for at, ref in enumerate((left_ref, mid_ref, right_ref)):
        for dx in range(3):
            shell[3 * dx + at] = ref[dx]

    def pairs(tile, sums):
        rows = [shell[4, comp, pl.ds(tile, 1), :] for comp in range(3)]
        columns = jnp.concatenate(rows + [jnp.zeros((5, 128), f32)], axis=0).T
        sources = []
        for entry in range(NB):
            code = listed[entry, tile]
            group = code >> 4
            layer = code & (TZ - 1)
            step_x = (group * 11) >> 5
            step_y = group - 3 * step_x
            step_z = (layer - tile + 1) & (TZ - 1)
            shifts = [(step - 1).astype(f32) for step in (step_x, step_y, step_z)]
            source = [shell[group, comp, pl.ds(layer, 1), :] for comp in range(4)]
            sources.append([source[comp] + shifts[comp] for comp in range(3)] + [source[3]])
        for chunk in range(16):
            part = slice(8 * chunk, 8 * chunk + 8)
            own = [jnp.broadcast_to(columns[part, comp : comp + 1], (8, 128)) for comp in range(3)]
            totals = [None] * 3
            for x, y, z, mass in sources:
                apart = [x - own[0], y - own[1], z - own[2]]
                square = apart[0] * apart[0] + apart[1] * apart[1] + apart[2] * apart[2]
                root = lax.rsqrt(square + softening)
                strength = (mass * jnp.exp(square * (-1.0 / split_scale))) * (root * root * root)
                for comp in range(3):
                    term = strength * apart[comp]
                    totals[comp] = term if totals[comp] is None else totals[comp] + term
            for comp in range(3):
                sums[128 * comp + 8 * chunk : 128 * comp + 8 * chunk + 8, :] = totals[comp]

    def add_up(tile, sums):
        ones = jnp.ones((8, 128), bf16)
        high, low = split(sums[...])
        total = dot_t(ones, high) + dot_t(ones, low)
        for comp in range(3):
            out_ref[comp, pl.ds(tile, 1), :] = total[:1, 128 * comp : 128 * comp + 128]

    def two(at, carry):
        add_up(2 * at, sums_even)
        pairs(2 * at + 1, sums_odd)
        add_up(2 * at + 1, sums_odd)
        pairs(2 * at + 2, sums_even)
        return carry

    pairs(0, sums_even)
    lax.fori_loop(0, TZ // 2 - 1, two, 0)
    add_up(TZ - 2, sums_even)
    pairs(TZ - 1, sums_odd)
    add_up(TZ - 1, sums_odd)


def call(kernel, shapes, operands, spaces="", scratch=(), cost=None, room=24 << 20):
    space_of = {"s": pltpu.SMEM, "h": pltpu.HBM, "a": pl.ANY, "v": pltpu.VMEM}
    spaces = spaces.ljust(len(operands), "v")
    shapes = [shape if isinstance(shape[0], tuple) else (shape, f32) for shape in shapes]
    return pl.pallas_call(
        kernel,
        out_shape=[jax.ShapeDtypeStruct(*shape) for shape in shapes],
        in_specs=[pl.BlockSpec(memory_space=space_of[space]) for space in spaces],
        out_specs=[pl.BlockSpec(memory_space=pltpu.VMEM)] * len(shapes),
        scratch_shapes=scratch,
        cost_estimate=cost,
        compiler_params=pltpu.CompilerParams(vmem_limit_bytes=room),
    )(*operands)


def exchange(value, axis):
    return lax.all_to_all(value, axis, split_axis=0, concat_axis=0, tiled=True)


def shift(value, axis, count, step):
    return lax.ppermute(value, axis, [(i, (i + step) % count) for i in range(count)])


def short_range(*operands):
    pairs = TZ * NB * 128 * 128
    return call(
        short_kernel,
        [(3, TZ, 128), ((2, TZ, 128, 128), bf16), (TZ, 16, 128)],
        operands,
        spaces="s",
        scratch=[pltpu.VMEM((9, 4, TZ, 128), f32)] + [pltpu.VMEM((3 * 128, 128), f32)] * 2,
        cost=pl.CostEstimate(flops=40_000 * pairs, bytes_accessed=400_000, transcendentals=2 * pairs),
    )


def shards(positions, masses, velocities, tile_counts, neighbour_list):
    t = tables()
    wide = ("gx", "gz")
    position = jnp.transpose(positions[0, 0], (1, 0, 2))
    velocity = jnp.transpose(velocities[0, 0], (1, 0, 2))
    mass = masses[0, 0]
    counts = tile_counts[0]
    listed = jnp.transpose(neighbour_list[0, 0], (1, 0))

    tile_shape = (4, TZ, 128)
    modes, packed, live = call(
        deposit_kernel,
        [(NY, 128), tile_shape, (TZ + PY, 128)],
        (counts, position, mass, t["fwd_z"], t["sine_z"]),
        spaces="hhhhh",
        scratch=[
            pltpu.SMEM((1, TZ), jnp.int32),
            pltpu.VMEM((3, TZ, 128), f32),
            pltpu.VMEM((TZ, 128), f32),
            pltpu.VMEM((8, 256, 256), bf16),
            pltpu.SemaphoreType.DMA((5,)),
        ],
        room=63_400_000,
    )
    modes = exchange(modes.reshape(PY, CY // 2, 2, 128), "gy").reshape(NY, 128)
    packed = packed.reshape(4 * TZ, 128)
    (modes,) = call(forward_y_kernel, [(4 * PX, 128)], (modes, *t["fwd_y"], packed))
    modes = exchange(modes.reshape(PX, 4, 128), wide).reshape(4 * PX, 128)
    waves = (t["kappa_x"], t["kappa_y"], t["kappa_z"])
    (fields,) = call(
        solve_x_kernel, [(7 * PX, 128)], (modes, *t["fwd_x"], *t["inv_x"], *waves)
    )
    fields = exchange(fields.reshape(PX, 7, 1, 128), wide).reshape(7 * PX, 128)
    fields, row = call(
        inverse_y_kernel,
        [(PY * 3 * CY, 128), (3, 4 * TZ, 128)],
        (fields, *t["inv_y"], packed),
    )
    row = row.reshape(3, 4, TZ, 128)
    left = shift(row, "gy", PY, 1)
    right = shift(row, "gy", PY, -1)
    fields = exchange(fields.reshape(PY, 3 * CY // 2, 2, 128), "gy").reshape(PY * 3 * CY, 128)
    short, deep, flat = short_range(listed, left, row, right)
    (kicked,) = call(
        kick_kernel,
        [(3, TZ, 128)],
        (live, fields, velocity, short, deep, flat, t["inv_z"]),
    )
    return jnp.transpose(kicked, (1, 0, 2))[None, None]


def solution(mesh):
    wide = ("gx", "gz")
    placed = (
        P(wide, "gy", None, None, None),
        P(wide, "gy", None, None),
        P(wide, "gy", None, None, None),
        P(wide, "gy", None),
        P(wide, "gy", None, None),
    )
    return jax.shard_map(
        shards,
        mesh=mesh,
        in_specs=placed,
        out_specs=P(wide, "gy", None, None, None),
        check_vma=False,
    )
```

```python
import functools

import jax
import jax.numpy as jnp
import ml_dtypes
import numpy as np
from jax import lax
from jax.experimental import pallas as pl
from jax.experimental.pallas import tpu as pltpu
from jax.sharding import PartitionSpec as P

CX = 2
CY = 6
NZ = 1024
TZ = 16
NB = 6
NX = 96
NY = 96
PX = 48
PY = 16
CELLS = NZ // TZ
BLOCK = NZ // PY
HALF = BLOCK // 2
REST = 4 * TZ - PX

smoothing = 0.1
screening = 0.01
split_scale = 2.0
softening = 0.05
long_kick = 1.0
short_kick = 0.05

f32 = jnp.float32
bf16 = jnp.bfloat16


def halves(table):
    high = table.astype(np.float32).astype(ml_dtypes.bfloat16)
    low = (table - high.astype(np.float64)).astype(np.float32).astype(ml_dtypes.bfloat16)
    return high, low


def real_basis(length, run):
    cells = np.arange(length)[:, None]
    wave = np.arange(length // 2)
    angle = 2 * np.pi * (cells * wave[None] % length) / length
    cosine = np.cos(angle) * np.sqrt(2 / length)
    sine = np.sin(angle) * np.sqrt(2 / length)
    step = np.sin(2 * np.pi * wave / length)
    cos_slope = sine * step
    sin_slope = -cosine * step
    cosine[:, 0] = np.sqrt(1 / length)
    sine[:, 0] = np.where(cells[:, 0] % 2 == 0, 1.0, -1.0) * np.sqrt(1 / length)
    cos_slope[:, 0] = 0
    sin_slope[:, 0] = 0
    kappa_cos = 4 * np.sin(np.pi * wave / length) ** 2
    kappa_sin = kappa_cos.copy()
    kappa_sin[0] = 4.0

    def laid(first, second):
        shape = first.shape[:-1] + (-1, 1, run)
        return np.concatenate([first.reshape(shape), second.reshape(shape)], axis=-2).reshape(
            first.shape[:-1] + (length,)
        )

    return (
        laid(cosine, sine),
        laid(cos_slope, sin_slope),
        laid(kappa_cos, kappa_sin),
        laid(-step, step),
    )


def depth_basis():
    table = np.zeros((4, 2, 128, 256))
    waves = np.zeros((4, 128))
    waves[0] = np.concatenate([8 * np.arange(64), 8 * np.arange(64) + 4])
    for residue in (1, 2, 3):
        waves[residue] = 8 * np.arange(128) + residue
    angle = 2 * np.pi * (np.arange(128)[:, None] * waves[:, None] % NZ) / NZ
    cosine = np.cos(angle) * np.sqrt(2 / NZ)
    sine = np.sin(angle) * np.sqrt(2 / NZ)
    cosine[0, :, 0] = np.sqrt(1 / NZ)
    sine[0, :, 0] = np.where(np.arange(128) % 2 == 0, 1.0, -1.0) * np.sqrt(1 / NZ)
    step = np.sin(2 * np.pi * waves / NZ)
    kappa_cos = 4 * np.sin(np.pi * waves / NZ) ** 2
    kappa_sin = kappa_cos.copy()
    step[0, 0] = 0
    kappa_sin[0, 0] = 4.0

    def laid(first, second):
        shape = first.shape[:-1] + (4, 1, HALF)
        return np.concatenate([first.reshape(shape), second.reshape(shape)], axis=-2).reshape(
            first.shape[:-1] + (256,)
        )

    table[:, 0] = laid(cosine, sine)
    table[:, 1] = laid(-sine, cosine)
    table[0, 1, :, 128:] = table[0, 0, :, 128:]
    table[0, 0, :, 128:] = 0
    table[0, 1, :, :128] = 0
    return (
        table.reshape(4, 256, 256),
        laid(kappa_cos, kappa_sin).reshape(NZ),
        laid(-step, step).reshape(NZ),
    )


ROOT_HALF = float(np.sqrt(0.5))
EXPONENT = float(-np.log2(np.e) / split_scale)


def waves_of(cells):
    total = [cells[a] + cells[a + 4] for a in range(4)]
    apart = [cells[a] - cells[a + 4] for a in range(4)]
    even, odd = total[0] + total[2], total[1] + total[3]
    less, more = (apart[1] - apart[3]) * ROOT_HALF, (apart[1] + apart[3]) * ROOT_HALF
    pairs = (
        (even + odd, even - odd),
        (apart[0] + less, more + apart[2]),
        (total[0] - total[2], total[1] - total[3]),
        (apart[0] - less, more - apart[2]),
    )
    return [jnp.concatenate(pair, axis=1) for pair in pairs]


def cells_of(pairs):
    (zero, four), one, two, three = [(pair[:, :128], pair[:, 128:]) for pair in pairs]
    plus, minus = zero + four, zero - four
    even = (plus + two[0], minus + two[1], plus - two[0], minus - two[1])
    less, more = (one[0] - three[0]) * ROOT_HALF, (one[1] + three[1]) * ROOT_HALF
    odd = (one[0] + three[0], more + less, one[1] - three[1], more - less)
    return [even[a] + odd[a] for a in range(4)] + [even[a] - odd[a] for a in range(4)]


@functools.lru_cache(None)
def tables():
    table_z, kappa_z, sine_z = depth_basis()
    basis_x, slope_x, kappa_x, _ = real_basis(NX, 1)
    basis_y, slope_y, kappa_y, _ = real_basis(NY, 1)
    out = {}
    out["fwd_z"] = np.concatenate(halves(table_z), axis=0)
    out["inv_z"] = np.concatenate(halves(table_z.transpose(0, 2, 1)), axis=0)
    out["fwd_y"] = halves(basis_y.T.reshape(PX, 2, NY).transpose(1, 0, 2).reshape(NY, NY))
    out["fwd_x"] = halves(basis_x.reshape(PX, CX, NX).transpose(2, 1, 0).reshape(NX, CX * PX))
    both = np.stack([slope_x.reshape(PX, CX, NX), basis_x.reshape(PX, CX, NX)])
    out["inv_x"] = halves(both.transpose(0, 2, 1, 3).reshape(2 * CX * PX, NX))

    rows = np.zeros((2, PY, 3, CY, 2, PX))
    spread = [table.reshape(PY, CY, PX, 2).transpose(3, 0, 1, 2) for table in (basis_y, slope_y)]
    rows[:, :, 0, :, 0] = spread[0]
    rows[:, :, 1, :, 1] = spread[1]
    rows[:, :, 2, :, 1] = spread[0]
    out["inv_y"] = halves(rows.reshape(2 * PY * 3 * CY, 2 * PX))
    out["kappa_x"] = kappa_x[:, None].astype(np.float32)
    out["kappa_y"] = np.repeat(kappa_y.reshape(PX, 2), BLOCK, axis=1).astype(np.float32)
    out["kappa_z"] = np.tile(kappa_z.reshape(PY, BLOCK), (1, 2)).astype(np.float32)
    out["sine_z"] = np.tile(sine_z.reshape(PY, BLOCK), (1, 2)).astype(np.float32)
    return out


def split(value):
    high = value.astype(bf16)
    return high, (value - high.astype(f32)).astype(bf16)


def dot(left, right):
    return lax.dot_general(left, right, (((1,), (0,)), ((), ())), preferred_element_type=f32)


def dot_t(left, right):
    return lax.dot_general(left, right, (((1,), (1,)), ((), ())), preferred_element_type=f32)


def table_dot(high_ref, low_ref, value):
    lanes = value.shape[1]
    high, low = split(value)
    both = dot(high_ref[...], jnp.concatenate([high, low], axis=1))
    return both[:, :lanes] + both[:, lanes:] + dot(low_ref[...], high)


def dot_table(value, table_ref, at):
    rows = value.shape[0]
    high, low = split(value)
    both = dot(jnp.concatenate([high, low], axis=0), table_ref[at])
    return both[:rows] + both[rows:] + dot(high, table_ref[4 + at])


def iota(shape, dim):
    return lax.broadcasted_iota(jnp.int32, shape, dim)


def plane_weights(pos_ref, tile):
    row = iota((16, 128), 0)
    row_x = (row >> 3).astype(f32)
    row_y = (row & 7).astype(f32)
    x = jnp.clip(pos_ref[0, tile : tile + 1, :] * CX - 0.5, 0.0, 1.0)
    y = jnp.clip(pos_ref[1, tile : tile + 1, :] * CY - 0.5, 0.0, CY - 1.0)
    return (1.0 - jnp.abs(x - row_x)) * jnp.maximum(1.0 - jnp.abs(y - row_y), 0.0)


def depth_weights(pos_ref, tile):
    z = (tile + pos_ref[2, tile : tile + 1, :]) * CELLS - 0.5 - (tile * CELLS - CELLS // 2)
    return jnp.maximum(1.0 - jnp.abs(z - iota((128, 128), 0).astype(f32)), 0.0)


def deposit_kernel(
    counts_hbm,
    pos_hbm,
    mass_hbm,
    table_hbm,
    sine_hbm,
    out_ref,
    packed_ref,
    live_ref,
    counts,
    pos_ref,
    mass_ref,
    table_ref,
    arrived,
):
    loads = [
        pltpu.make_async_copy(source, held, arrived.at[at])
        for at, (source, held) in enumerate(
            (
                (counts_hbm, counts),
                (pos_hbm, pos_ref),
                (mass_hbm, mass_ref),
                (table_hbm, table_ref),
                (sine_hbm, live_ref.at[TZ : TZ + PY]),
            )
        )
    ]
    for load in loads:
        load.start()
    for load in loads[:3]:
        load.wait()
    packed_ref[:3] = pos_ref[...]
    slot = iota((1, 128), 1)
    windows = []
    for tile in range(TZ):
        live = slot < counts[0, tile]
        live_ref[tile : tile + 1, :] = jnp.where(live, 1.0, 0.0)
        mass = jnp.where(live, mass_ref[tile : tile + 1, :], 0.0)
        packed_ref[3, tile : tile + 1, :] = mass
        flat_high, flat_low = split(plane_weights(pos_ref, tile) * mass)
        deep_high, deep_low = split(depth_weights(pos_ref, tile))
        both = dot_t(jnp.concatenate([flat_high, flat_low], axis=0), deep_high)
        windows.append(both[:16] + both[16:] + dot_t(flat_high, deep_low))
    even = jnp.concatenate(windows[0::2], axis=1)
    odd = jnp.concatenate(windows[1::2], axis=1)
    density = pltpu.roll(even, NZ - CELLS // 2, 1) + pltpu.roll(odd, CELLS // 2, 1)
    pairs = waves_of([density[:, 128 * a : 128 * a + 128] for a in range(8)])
    for load in loads[3:]:
        load.wait()
    modes = [dot_table(value, table_ref, at) for at, value in enumerate(pairs)]
    first = iota((8, 128), 1) < BLOCK
    for pair in range(PY // 2):
        part = modes[pair // 2][:, 128 * (pair % 2) : 128 * (pair % 2) + 128]
        near = part[:8]
        far = part[8:]
        blocks = (
            jnp.where(first, near, pltpu.roll(far, BLOCK, 1)),
            jnp.where(first, pltpu.roll(near, BLOCK, 1), far),
        )
        for at, block in enumerate(blocks):
            start = CY * (2 * pair + at)
            out_ref[start : start + CY, :] = block[:CY]


def forward_y_kernel(in_ref, high_ref, low_ref, packed_ref, out_ref):
    value = table_dot(high_ref, low_ref, in_ref[...])
    for at in range(2):
        out_ref[pl.ds(at, PX, stride=4), :] = value[PX * at : PX * (at + 1)]
        out_ref[pl.ds(3 + 4 * at, REST, stride=8), :] = packed_ref[PX:, :]
    out_ref[pl.ds(2, PX, stride=4), :] = packed_ref[:PX, :]
    out_ref[pl.ds(8 * REST + 3, PX - 2 * REST, stride=4), :] = jnp.zeros((PX - 2 * REST, 128), f32)


def solve_x_kernel(
    in_ref, fwd_high, fwd_low, inv_high, inv_low, kappa_x, kappa_y, kappa_z, out_ref
):
    at_x = lax.axis_index(("gx", "gz"))
    at_y = lax.axis_index("gy")
    first = iota((PX, 128), 1) < BLOCK
    wave_a = in_ref[pl.ds(0, PX, stride=4), :]
    wave_b = in_ref[pl.ds(1, PX, stride=4), :]
    cells_0 = jnp.where(first, wave_a, pltpu.roll(wave_b, BLOCK, 1))
    cells_1 = jnp.where(first, pltpu.roll(wave_a, BLOCK, 1), wave_b)
    spectrum = table_dot(fwd_high, fwd_low, jnp.concatenate([cells_0, cells_1], axis=0))
    kappa_sum = kappa_x[...] + (kappa_y[pl.ds(at_x, 1), :] + kappa_z[pl.ds(at_y, 1), :])
    potential = spectrum * (-jnp.exp(-smoothing * kappa_sum) / (kappa_sum + screening))
    fields = table_dot(inv_high, inv_low, potential)
    for at in range(4):
        out_ref[pl.ds(at, PX, stride=7), :] = fields[PX * at : PX * (at + 1)]
    piece = in_ref[pl.ds(2, PX, stride=4), :]
    out_ref[pl.ds(4, PX, stride=7), :] = pltpu.roll(piece, 1, 0)
    out_ref[pl.ds(5, PX, stride=7), :] = pltpu.roll(piece, PX - 1, 0)
    near = in_ref[pl.ds(3, PX, stride=4), :]
    far = pltpu.roll(near, BLOCK, 1)
    even = at_x % 2 == 0
    out_ref[pl.ds(6, PX, stride=7), :] = jnp.where(
        first,
        pltpu.roll(jnp.where(even, near, far), 1, 0),
        pltpu.roll(jnp.where(even, far, near), PX - 1, 0),
    )


def inverse_y_kernel(in_ref, high_ref, low_ref, packed_ref, out_ref, row_ref):
    rows = PY * 3 * CY
    first = iota((rows, 128), 1) < BLOCK
    cells = [
        jnp.concatenate([in_ref[pl.ds(at, PX, stride=7), :] for at in (x, x + 2)], axis=0)
        for x in range(CX)
    ]
    value = table_dot(high_ref, low_ref, jnp.concatenate(cells, axis=1))
    cos_0, cos_1 = value[:rows, :128], value[:rows, 128:]
    sin_0, sin_1 = value[rows:, :128], value[rows:, 128:]
    cell_0 = cos_0 + pltpu.roll(sin_0, BLOCK, 1)
    cell_1 = pltpu.roll(cos_1, BLOCK, 1) + sin_1
    out_ref[...] = jnp.where(first, cell_0, cell_1)
    row_ref[1] = packed_ref[...]
    row_ref[0, :PX, :] = in_ref[pl.ds(4, PX, stride=7), :]
    row_ref[2, :PX, :] = in_ref[pl.ds(5, PX, stride=7), :]
    low_half = first[:REST]
    one, two = in_ref[pl.ds(6, REST, stride=14), :], in_ref[pl.ds(13, REST, stride=14), :]
    row_ref[0, PX:, :] = jnp.where(low_half, one, pltpu.roll(two, BLOCK, 1))
    row_ref[2, PX:, :] = jnp.where(low_half, pltpu.roll(one, BLOCK, 1), two)


def kick_kernel(
    live_ref, in_ref, vel_ref, short_ref, deep_ref, flat_ref, table_ref, out_ref
):
    first = iota((24, 128), 1) < BLOCK
    cosines = (iota((8, 128), 1) & (BLOCK - 1)) < HALF

    def block(at):
        last = PY * 3 * CY - 8
        parts = []
        for row in range(3 * CY * at, 3 * CY * (at + 1), CY):
            part = in_ref[min(row, last) : min(row, last) + 8, :]
            parts.append(part if row <= last else pltpu.roll(part, 8 - (row - last), 0))
        turned = jnp.where(
            cosines, pltpu.roll(parts[2], 128 - HALF, 1), pltpu.roll(parts[2], HALF, 1)
        )
        return jnp.concatenate(parts[:2] + [turned * live_ref[TZ + at : TZ + at + 1, :]], axis=0)

    near, far = [], []
    for pair in range(PY // 2):
        a, b = block(2 * pair), block(2 * pair + 1)
        near.append(jnp.where(first, a, pltpu.roll(b, BLOCK, 1)))
        far.append(jnp.where(first, pltpu.roll(a, BLOCK, 1), b))
    modes = [jnp.concatenate(parts, axis=0) for parts in zip(near, far)]
    pairs = [
        dot_table(jnp.concatenate(modes[2 * at : 2 * at + 2], axis=1), table_ref, at)
        for at in range(4)
    ]
    forces = jnp.concatenate(cells_of(pairs), axis=1)
    shifted = (
        pltpu.roll(forces, CELLS // 2, 1),
        pltpu.roll(forces, NZ - CELLS // 2, 1),
    )
    for tile in range(TZ):
        start = 128 * (tile // 2)
        window = shifted[tile % 2][:, start : start + 128]
        high, low = split(window)
        both = dot(jnp.concatenate([high, low], axis=0), deep_ref[0, tile])
        picked = both[:48] + both[48:] + dot(high, deep_ref[1, tile])
        flat = flat_ref[tile]
        live = live_ref[tile : tile + 1, :]
        for comp in range(3):
            at = 8 * comp
            total = flat[:8] * picked[at : at + 8] + flat[8:] * picked[24 + at : 32 + at]
            long_accel = jnp.sum(total, axis=0, keepdims=True)
            kick = long_kick * long_accel + short_kick * short_ref[comp, tile : tile + 1, :]
            out_ref[comp, tile : tile + 1, :] = vel_ref[comp, tile : tile + 1, :] + live * kick


def short_kernel(
    listed, left_ref, mid_ref, right_ref, out_ref, deep_ref, flat_ref, shell, sums_even, sums_odd
):
    pos_ref = mid_ref.at[1]
    for tile in range(TZ):
        flat_ref[tile] = plane_weights(pos_ref, tile)
        deep_ref[0, tile], deep_ref[1, tile] = split(depth_weights(pos_ref, tile))
    for at, ref in enumerate((left_ref, mid_ref, right_ref)):
        for dx in range(3):
            shell[3 * dx + at] = ref[dx]

    def pairs(tile, sums):
        rows = [shell[4, comp, pl.ds(tile, 1), :] for comp in range(3)]
        columns = jnp.concatenate(rows + [jnp.zeros((5, 128), f32)], axis=0).T
        sources = []
        for entry in range(NB):
            code = listed[entry, tile]
            group = code >> 4
            layer = code & (TZ - 1)
            step_x = (group * 11) >> 5
            step_y = group - 3 * step_x
            step_z = (layer - tile + 1) & (TZ - 1)
            shifts = [(step - 1).astype(f32) for step in (step_x, step_y, step_z)]
            source = [shell[group, comp, pl.ds(layer, 1), :] for comp in range(4)]
            sources.append([source[comp] + shifts[comp] for comp in range(3)] + [source[3]])
        for chunk in range(16):
            part = slice(8 * chunk, 8 * chunk + 8)
            own = [jnp.broadcast_to(columns[part, comp : comp + 1], (8, 128)) for comp in range(3)]
            totals = [None] * 3
            for x, y, z, mass in sources:
                apart = [x - own[0], y - own[1], z - own[2]]
                square = apart[0] * apart[0] + apart[1] * apart[1] + apart[2] * apart[2]
                root = lax.rsqrt(square + softening)
                strength = (mass * jnp.exp2(square * EXPONENT)) * (root * root * root)
                for comp in range(3):
                    term = strength * apart[comp]
                    totals[comp] = term if totals[comp] is None else totals[comp] + term
            for comp in range(3):
                sums[128 * comp + 8 * chunk : 128 * comp + 8 * chunk + 8, :] = totals[comp]

    def add_up(tile, sums):
        ones = jnp.ones((8, 128), bf16)
        high, low = split(sums[...])
        total = dot_t(ones, high) + dot_t(ones, low)
        for comp in range(3):
            out_ref[comp, pl.ds(tile, 1), :] = total[:1, 128 * comp : 128 * comp + 128]

    def two(at, carry):
        add_up(2 * at, sums_even)
        pairs(2 * at + 1, sums_odd)
        add_up(2 * at + 1, sums_odd)
        pairs(2 * at + 2, sums_even)
        return carry

    pairs(0, sums_even)
    lax.fori_loop(0, TZ // 2 - 1, two, 0)
    add_up(TZ - 2, sums_even)
    pairs(TZ - 1, sums_odd)
    add_up(TZ - 1, sums_odd)


def call(kernel, shapes, operands, spaces="", scratch=(), cost=None, room=24 << 20):
    space_of = {"s": pltpu.SMEM, "h": pltpu.HBM, "a": pl.ANY, "v": pltpu.VMEM}
    spaces = spaces.ljust(len(operands), "v")
    shapes = [shape if isinstance(shape[0], tuple) else (shape, f32) for shape in shapes]
    return pl.pallas_call(
        kernel,
        out_shape=[jax.ShapeDtypeStruct(*shape) for shape in shapes],
        in_specs=[pl.BlockSpec(memory_space=space_of[space]) for space in spaces],
        out_specs=[pl.BlockSpec(memory_space=pltpu.VMEM)] * len(shapes),
        scratch_shapes=scratch,
        cost_estimate=cost,
        compiler_params=pltpu.CompilerParams(vmem_limit_bytes=room),
    )(*operands)


def exchange(value, axis):
    return lax.all_to_all(value, axis, split_axis=0, concat_axis=0, tiled=True)


def shift(value, axis, count, step):
    return lax.ppermute(value, axis, [(i, (i + step) % count) for i in range(count)])


def short_range(*operands):
    pairs = TZ * NB * 128 * 128
    return call(
        short_kernel,
        [(3, TZ, 128), ((2, TZ, 128, 128), bf16), (TZ, 16, 128)],
        operands,
        spaces="s",
        scratch=[pltpu.VMEM((9, 4, TZ, 128), f32)] + [pltpu.VMEM((3 * 128, 128), f32)] * 2,
        cost=pl.CostEstimate(flops=40_000 * pairs, bytes_accessed=400_000, transcendentals=2 * pairs),
    )


def shards(positions, masses, velocities, tile_counts, neighbour_list):
    t = tables()
    wide = ("gx", "gz")
    position = jnp.transpose(positions[0, 0], (1, 0, 2))
    velocity = jnp.transpose(velocities[0, 0], (1, 0, 2))
    mass = masses[0, 0]
    counts = tile_counts[0]
    listed = jnp.transpose(neighbour_list[0, 0], (1, 0))

    tile_shape = (4, TZ, 128)
    modes, packed, live = call(
        deposit_kernel,
        [(NY, 128), tile_shape, (TZ + PY, 128)],
        (counts, position, mass, t["fwd_z"], t["sine_z"]),
        spaces="hhhhh",
        scratch=[
            pltpu.SMEM((1, TZ), jnp.int32),
            pltpu.VMEM((3, TZ, 128), f32),
            pltpu.VMEM((TZ, 128), f32),
            pltpu.VMEM((8, 256, 256), bf16),
            pltpu.SemaphoreType.DMA((5,)),
        ],
        room=63_400_000,
    )
    modes = exchange(modes.reshape(PY, CY // 2, 2, 128), "gy").reshape(NY, 128)
    packed = packed.reshape(4 * TZ, 128)
    (modes,) = call(forward_y_kernel, [(4 * PX, 128)], (modes, *t["fwd_y"], packed))
    modes = exchange(modes.reshape(PX, 4, 128), wide).reshape(4 * PX, 128)
    waves = (t["kappa_x"], t["kappa_y"], t["kappa_z"])
    (fields,) = call(
        solve_x_kernel, [(7 * PX, 128)], (modes, *t["fwd_x"], *t["inv_x"], *waves)
    )
    fields = exchange(fields.reshape(PX, 7, 1, 128), wide).reshape(7 * PX, 128)
    fields, row = call(
        inverse_y_kernel,
        [(PY * 3 * CY, 128), (3, 4 * TZ, 128)],
        (fields, *t["inv_y"], packed),
    )
    row = row.reshape(3, 4, TZ, 128)
    left = shift(row, "gy", PY, 1)
    right = shift(row, "gy", PY, -1)
    fields = exchange(fields.reshape(PY, 3 * CY // 2, 2, 128), "gy").reshape(PY * 3 * CY, 128)
    short, deep, flat = short_range(listed, left, row, right)
    (kicked,) = call(
        kick_kernel,
        [(3, TZ, 128)],
        (live, fields, velocity, short, deep, flat, t["inv_z"]),
    )
    return jnp.transpose(kicked, (1, 0, 2))[None, None]


def solution(mesh):
    wide = ("gx", "gz")
    placed = (
        P(wide, "gy", None, None, None),
        P(wide, "gy", None, None),
        P(wide, "gy", None, None, None),
        P(wide, "gy", None),
        P(wide, "gy", None, None),
    )
    return jax.shard_map(
        shards,
        mesh=mesh,
        in_specs=placed,
        out_specs=P(wide, "gy", None, None, None),
        check_vma=False,
    )
```
